256 devices in a mesh: pool: 64 (over y, z, core), tp: 4 (over x).
Axes of the slice: x: 4, y: 4, z: 8, core: 2. Of those that a mesh axis runs over, the one named last changes fastest.
Arguments:
- normed_input: bfloat16 [2, 3072, 8192], P(None, 'pool', 'tp'), may hold values from -6 to 6
- base_query_output: bfloat16 [2, 3072, 8192], P(None, 'pool', 'tp'), may hold values from -4.5 to 4.5
- adapter_down_weight: bfloat16 [8192, 512, 64], P('tp', 'pool'), may hold values from -0.0625 to 0.0625
- adapter_up_weight: bfloat16 [512, 64, 8192], P('pool', None, 'tp'), may hold values from -0.75 to 0.75
- row_adapter_index: int32 [3072], P('pool'), may hold values from 0 to 511, as said below
- paged_key_cache: bfloat16 [12288, 32, 8, 128], P('pool', None, 'tp'), may hold values from -4.5 to 4.5
- paged_value_cache: bfloat16 [12288, 32, 8, 128], P('pool', None, 'tp'), may hold values from -6 to 6
- step_token_keys: bfloat16 [2, 3072, 8, 128], P(None, 'pool', 'tp'), may hold values from -6 to 6
- step_token_values: bfloat16 [2, 3072, 8, 128], P(None, 'pool', 'tp'), may hold values from -6 to 6
- row_page_table: int32 [3072, 4], P('pool'), may hold values from 0 to 191, as said below
- lengths: int32 [3072], P('pool'), may hold values from 1 to 128, as said below
Outputs:
- attended: bfloat16 [2, 3072, 8192], P(None, 'pool', 'tp')
The draws below stay inside these ranges and needn't reach their ends.
Inputs may be any that keep to these rules, and one draw needn't show every extreme that they name: Adapter ids name the pool index row_adapter_index // 8; among the rows of one device at most 2 name adapters of one pool index, and in every device some 2 rows do. `row_page_table`: each device's rows of the table hold each of its 192 pages exactly once. `lengths`: every device has a row with 128 cached tokens.
All inputs are finite; a program needn't handle non-finite values.
Results may differ from the reference program's by a relative error of at most 0.0059.
Values may be sent and summed in bfloat16 or wider, within the bound.
A program may use at most 64 MiB of HBM per device.

```python
import jax
import jax.numpy as jnp
from jax import lax

MODEL_WIDTH = 8192
QUERY_HEADS = 64
KV = 8
HEAD_SIZE = 128
ADAPTER_RANK = 64
ADP_DEV = 8
ROWS_DEV = 48
CTX = 128
PAGE = 32
MAXP = 4
PAGES_DEV = 192
PAGES = 12288
ROWS = 3072
ADAPTER_COUNT = 512
N_POOL = 64


def draw_base_query_output(key, part):
    key = jax.random.fold_in(key, 11)
    values = jnp.clip(jax.random.normal(key, (2, ROWS, QUERY_HEADS * HEAD_SIZE), jnp.float32), -4.5, 4.5)
    return values.astype(jnp.bfloat16)


def draw_paged_key_cache(key, part):
    key = jax.random.fold_in(key, 12)
    values = jnp.clip(jax.random.normal(key, (PAGES, PAGE, KV, HEAD_SIZE), jnp.float32), -4.5, 4.5)
    return values.astype(jnp.bfloat16)


def draw_row_adapter_index(key, part):
    key = jax.random.fold_in(key, 3)

    def block(index):
        sub = jax.random.fold_in(key, index)
        first, second, third = jax.random.split(sub, 3)
        owners = jax.random.permutation(first, N_POOL)
        place = jnp.maximum(jnp.arange(ROWS_DEV, dtype=jnp.int32) - 1, 0) % N_POOL
        owner = owners[place]
        owner = owner[jax.random.permutation(second, ROWS_DEV)]
        local = jax.random.randint(third, (ROWS_DEV,), 0, ADP_DEV)
        return (owner * ADP_DEV + local).astype(jnp.int32)
    return jax.vmap(block)(jnp.arange(N_POOL, dtype=jnp.int32)).reshape(ROWS)


def draw_row_page_table(key, part):
    key = jax.random.fold_in(key, 4)

    def block(index):
        sub = jax.random.fold_in(key, index)
        return jax.random.permutation(sub, PAGES_DEV).astype(jnp.int32).reshape(ROWS_DEV, MAXP)
    return jax.vmap(block)(jnp.arange(N_POOL, dtype=jnp.int32)).reshape(ROWS, MAXP)


def draw_lengths(key, part):
    key = jax.random.fold_in(key, 5)

    def block(index):
        sub = jax.random.fold_in(key, index)
        first, second = jax.random.split(sub)
        counts = jax.random.randint(first, (ROWS_DEV,), 1, CTX + 1)
        chosen = jax.random.randint(second, (), 0, ROWS_DEV)
        return jnp.where(jnp.arange(ROWS_DEV, dtype=jnp.int32) == chosen, CTX, counts).astype(jnp.int32)
    return jax.vmap(block)(jnp.arange(N_POOL, dtype=jnp.int32)).reshape(ROWS)


def steps_of(rng, extent, cuts, smallest, top_value):
    factor_of, own = 1.0, jax.random.fold_in(rng, 6)
    for position, parts in cuts:
        draws = jnp.exp(jax.random.uniform(jax.random.fold_in(own, position), (parts,), jnp.float32, smallest / len(cuts), top_value / len(cuts)))
        factor_of = factor_of * jnp.repeat(draws, extent[position] // parts).reshape([-1 if axis == position else 1 for axis in range(len(extent))])
    return factor_of


def normal_values(key, extent, spread, bound, cuts=(), kind=jnp.bfloat16):
    result = jax.random.normal(key, extent, jnp.float32) * spread
    if len(cuts) > 0:
        result = steps_of(key, extent, cuts, -0.22, 0.18) * result
    return jnp.clip(result, min=-bound, max=bound).astype(kind)


def setup_inputs(seed: int = 0) -> dict:
    key_list = jax.random.split(jax.random.key(seed), 12)
    normed_input = normal_values(key_list[0], (2, ROWS, MODEL_WIDTH), 1.0, 6.0, ((1, 64), (2, 4)))
    base_query_output = draw_base_query_output(jax.random.fold_in(key_list[11], 71), 0)
    adapter_down_weight = normal_values(key_list[2], (MODEL_WIDTH, ADAPTER_COUNT, ADAPTER_RANK), MODEL_WIDTH ** -0.5, 0.0625, ((0, 4), (1, 64)))
    adapter_up_weight = normal_values(key_list[3], (ADAPTER_COUNT, ADAPTER_RANK, QUERY_HEADS * HEAD_SIZE), ADAPTER_RANK ** -0.5, 0.75, ((0, 64), (2, 4)))
    row_adapter_index = draw_row_adapter_index(jax.random.fold_in(key_list[11], 71), 0)
    paged_key_cache = draw_paged_key_cache(jax.random.fold_in(key_list[11], 71), 0)
    paged_value_cache = normal_values(key_list[6], (PAGES, PAGE, KV, HEAD_SIZE), 1.0, 6.0, ((0, 64), (2, 4)))
    step_token_keys = normal_values(key_list[7], (2, ROWS, KV, HEAD_SIZE), 1.0, 6.0, ((1, 64), (2, 4)))
    step_token_values = normal_values(key_list[8], (2, ROWS, KV, HEAD_SIZE), 1.0, 6.0, ((1, 64), (2, 4)))
    row_page_table = draw_row_page_table(jax.random.fold_in(key_list[11], 71), 0)
    lengths = draw_lengths(jax.random.fold_in(key_list[11], 71), 0)
    return dict(normed_input=normed_input, base_query_output=base_query_output, adapter_down_weight=adapter_down_weight, adapter_up_weight=adapter_up_weight, row_adapter_index=row_adapter_index, paged_key_cache=paged_key_cache, paged_value_cache=paged_value_cache, step_token_keys=step_token_keys, step_token_values=step_token_values, row_page_table=row_page_table, lengths=lengths)


ADAPTER_SCALE = 0.5

def adapter_row_update(input_row, identity_matrix, adapter_down_weight, adapter_up_weight):
    down_output = lax.dynamic_index_in_dim(adapter_down_weight, identity_matrix, 1, keepdims=False)
    update_row = jnp.dot(input_row[None, :], down_output, preferred_element_type=jnp.float32)[0].astype(jnp.bfloat16)
    up_output = lax.dynamic_index_in_dim(adapter_up_weight, identity_matrix, 0, keepdims=False)
    query_correction = jnp.dot(update_row[None, :], up_output, preferred_element_type=jnp.float32)[0] * ADAPTER_SCALE
    return query_correction.astype(jnp.bfloat16)

def attend_row(query, keys, values, extra_keys, extra_values, length):
    kvn = keys.shape[1]
    head = keys.shape[2]
    inv = 1.0 / jnp.sqrt(jnp.float32(head))
    grouped = query.reshape(kvn, -1, head).astype(jnp.float32)
    s_old = jnp.einsum('kgh,tkh->kgt', grouped, keys.astype(jnp.float32)) * inv
    live = jnp.arange(keys.shape[0], dtype=jnp.int32) < length
    s_old = jnp.where(live[None, None, :], s_old, jnp.float32(-1e+30))
    s_new = jnp.einsum('kgh,ekh->kge', grouped, extra_keys.astype(jnp.float32)) * inv
    top = jnp.maximum(lax.optimization_barrier(jnp.max(s_old, axis=-1)), lax.optimization_barrier(jnp.max(s_new, axis=-1)))[..., None]
    e_old = jnp.exp(s_old - top)
    e_new = jnp.exp(s_new - top)
    total = lax.optimization_barrier(jnp.sum(e_old, axis=-1, keepdims=True)) + lax.optimization_barrier(jnp.sum(e_new, axis=-1, keepdims=True))
    p_old = (e_old / total).astype(jnp.bfloat16).astype(jnp.float32)
    p_new = (e_new / total).astype(jnp.bfloat16).astype(jnp.float32)
    out = jnp.einsum('kgt,tkh->kgh', p_old, values.astype(jnp.float32))
    out = out + jnp.einsum('kge,ekh->kgh', p_new, extra_values.astype(jnp.float32))
    return out.reshape(-1).astype(jnp.bfloat16)

def reference(normed_input, base_query_output, adapter_down_weight, adapter_up_weight, row_adapter_index, paged_key_cache, paged_value_cache, step_token_keys, step_token_values, row_page_table, lengths):
    row_index = jnp.arange(ROWS, dtype=jnp.int32)
    results = []
    for decode_step in range(2):

        def one_row(args):
            input_row, identity_matrix = args
            return adapter_row_update(input_row, identity_matrix, adapter_down_weight, adapter_up_weight)
        query_correction = lax.map(one_row, (normed_input[decode_step], row_adapter_index))
        query = (base_query_output[decode_step].astype(jnp.float32) + query_correction.astype(jnp.float32)).astype(jnp.bfloat16)

        def attend_one(row):
            pages = row_page_table[row] + row // ROWS_DEV * PAGES_DEV
            keys = paged_key_cache[pages].reshape(CTX, KV, HEAD_SIZE)
            values = paged_value_cache[pages].reshape(CTX, KV, HEAD_SIZE)
            extra_keys = step_token_keys[:decode_step + 1, row]
            extra_values = step_token_values[:decode_step + 1, row]
            return attend_row(query[row], keys, values, extra_keys, extra_values, lengths[row])
        results.append(lax.map(attend_one, row_index))
    return jnp.stack(results, axis=0)
```

```python
import functools

import jax
import jax.numpy as jnp
from jax import lax
from jax.experimental import pallas as pl
from jax.experimental.pallas import tpu as pltpu
from jax.sharding import PartitionSpec as P

ADAPTER_SCALE = 0.5
MESH = pl.DeviceIdType.MESH
Y, Z, C = 4, 8, 2
POOL = Y * Z * C
TP = 4
GROUP = 8
GROUPS = POOL // GROUP
STEPS = 2
SLOTS = 2
PER = STEPS * SLOTS
BLOCK = 16
LANES = 128


def offsets(k):
    return k // (Z * C), k % Z, (k // Z) % C


def ahead(me, k):
    dy, dz, dc = offsets(k)
    y, z, c = me // (Z * C), (me // C) % Z, me % C
    return (((y + dy) % Y) * Z + (z + dz) % Z) * C + (c + dc) % C


def behind(me, k):
    dy, dz, dc = offsets(k)
    y, z, c = me // (Z * C), (me // C) % Z, me % C
    return (((y + Y - dy) % Y) * Z + (z + Z - dz) % Z) * C + (c + C - dc) % C


def position(me, other):
    y, z, c = me // (Z * C), (me // C) % Z, me % C
    oy, oz, oc = other // (Z * C), (other // C) % Z, other % C
    dy, dz, dc = (oy - y + Y) % Y, (oz - z + Z) % Z, (oc - c + C) % C
    return (dy * C + dc) * Z + dz


def kernel(
    rows,
    ctx,
    page,
    slot_row,
    row_answer,
    pages,
    lengths,
    picks,
    x_hbm,
    base_hbm,
    down_hbm,
    up_hbm,
    key_hbm,
    value_hbm,
    new_key_hbm,
    new_value_hbm,
    out_ref,
    x_in,
    base_in,
    down,
    up,
    keys,
    values,
    new_keys,
    new_values,
    x_blocks,
    base_blocks,
    out_blocks,
    sent,
    got,
    got_picks,
    masks,
    own_part,
    parts,
    wide,
    answers,
    returned,
    local_sems,
    x_send,
    x_recv,
    pick_send,
    pick_recv,
    part_send,
    part_recv,
    answer_send,
    answer_recv,
):
    me = lax.axis_index("pool")
    my_tp = lax.axis_index("tp")
    heads = BLOCK
    f32, bf16 = jnp.float32, jnp.bfloat16

    barrier = pltpu.get_barrier_semaphore()

    def greet(k, _):
        pl.semaphore_signal(
            barrier, inc=1, device_id={"pool": ahead(me, k)}, device_id_type=MESH
        )
        return 0

    lax.fori_loop(1, POOL, greet, 0)
    for t in range(1, TP):
        pl.semaphore_signal(
            barrier, inc=1, device_id={"tp": (my_tp + t) % TP}, device_id_type=MESH
        )

    loads = [
        pltpu.make_async_copy(src, dst, local_sems.at[i])
        for i, (src, dst) in enumerate(
            (
                (x_hbm, x_in),
                (down_hbm, down),
                (up_hbm, up),
                (base_hbm, base_in),
                (key_hbm, keys),
                (value_hbm, values),
                (new_key_hbm, new_keys),
                (new_value_hbm, new_values),
            )
        )
    ]
    for load in loads:
        load.start()

    def to_blocks(src, dst):
        for s in range(STEPS):
            for c in range(BLOCK):
                dst[pl.ds(s * rows * BLOCK + c, rows, stride=BLOCK), :] = src[
                    s, :, c * LANES : (c + 1) * LANES
                ].astype(f32)

    loads[0].wait()
    to_blocks(x_in, base_blocks)
    x_blocks[...] = base_blocks[...].astype(bf16).reshape(STEPS * rows, BLOCK, LANES)

    pl.semaphore_wait(barrier, POOL - 1 + TP - 1)

    def message(k, src, dst, send_sem, recv_sem, to):
        return pltpu.make_async_remote_copy(
            src_ref=src.at[pl.ds(k * PER, PER)],
            dst_ref=dst.at[pl.ds(k * PER, PER)],
            send_sem=send_sem,
            recv_sem=recv_sem,
            device_id={"pool": to},
            device_id_type=MESH,
        )

    def blocks_of(k, dst):
        for j in range(SLOTS):
            row = slot_row[k * SLOTS + j]
            for s in range(STEPS):
                dst[k * PER + s * SLOTS + j] = x_blocks[row + s * rows]

    def send_row(k, _):
        blocks_of(k, sent)
        to = ahead(me, k)
        pltpu.make_async_remote_copy(
            src_ref=picks.at[k],
            dst_ref=got_picks.at[k],
            send_sem=pick_send,
            recv_sem=pick_recv.at[k // GROUP],
            device_id={"pool": to},
            device_id_type=MESH,
        ).start()
        message(k, sent, got, x_send, x_recv.at[k // GROUP], to).start()
        return 0

    lax.fori_loop(1, POOL, send_row, 0)
    blocks_of(0, got)
    got_picks[0] = picks[0]

    loads[1].wait()
    loads[2].wait()

    grows = GROUP * PER
    width = down.shape[0]
    rank = width // 8
    spread = (
        lax.broadcasted_iota(jnp.int32, (grows, GROUP), 0) // PER
        == lax.broadcasted_iota(jnp.int32, (grows, GROUP), 1)
    ).astype(f32)
    lane = lax.broadcasted_iota(jnp.int32, (grows, LANES), 1)
    slot = lax.broadcasted_iota(jnp.int32, (grows, LANES), 0) % SLOTS
    slot_lanes = (lane // 8 == slot).astype(f32)
    widen = (
        lax.broadcasted_iota(jnp.int32, (LANES, width), 0) % 8
        == lax.broadcasted_iota(jnp.int32, (LANES, width), 1) // rank
    ).astype(f32)

    def group_bytes(g, first, ref, per, sem):
        lo, n = g * GROUP * per, GROUP * per
        if first:
            lo, n = per, (GROUP - 1) * per
        part = ref.at[pl.ds(lo, n)]
        pltpu.make_async_copy(part, part, sem).wait()

    def project_down(g, first):
        group_bytes(g, first, got, PER, x_recv.at[g])
        group_bytes(g, first, got_picks, 1, pick_recv.at[g])
        wide[...] = got[pl.ds(g * grows, grows)].reshape(grows * BLOCK, LANES).astype(f32)
        features = jnp.concatenate(
            [wide[pl.ds(c, grows, stride=BLOCK), :] for c in range(BLOCK)], axis=1
        ).astype(bf16)
        product = lax.dot_general(
            features, down[...], (((1,), (1,)), ((), ())), preferred_element_type=f32
        )
        chosen = got_picks[pl.ds(g * GROUP, GROUP)].reshape(GROUP, LANES)
        chosen = jnp.dot(spread, chosen, preferred_element_type=f32) * slot_lanes
        mask = jnp.dot(chosen, widen, preferred_element_type=f32)
        masks[g] = mask.astype(bf16)
        product = product * mask
        part = product[:, :LANES]
        for i in range(1, width // LANES):
            part = part + product[:, i * LANES : (i + 1) * LANES]
        own_part[g] = part
        for t in range(1, TP):
            pltpu.make_async_remote_copy(
                src_ref=own_part.at[g],
                dst_ref=parts.at[g, t - 1],
                send_sem=part_send,
                recv_sem=part_recv.at[g],
                device_id={"tp": (my_tp + t) % TP},
                device_id_type=MESH,
            ).start()

    def project_up(g, first):
        pltpu.make_async_copy(parts.at[g], parts.at[g], part_recv.at[g]).wait()
        u = own_part[g] + parts[g, 0] + parts[g, 1] + parts[g, 2]
        u = u.astype(bf16)
        u = jnp.concatenate([u] * (width // LANES), axis=1) * masks[g]
        delta = jnp.dot(u, up[...], preferred_element_type=f32) * ADAPTER_SCALE
        for c in range(BLOCK):
            wide[pl.ds(c, grows, stride=BLOCK), :] = delta[:, c * LANES : (c + 1) * LANES]
        answers[pl.ds(g * grows, grows)] = (
            wide[...].astype(bf16).reshape(grows, BLOCK, LANES)
        )

        def answer(k, _):
            message(k, answers, returned, answer_send, answer_recv, behind(me, k)).start()
            return 0

        if first:
            returned[pl.ds(0, PER)] = answers[pl.ds(0, PER)]
            lax.fori_loop(1, GROUP, answer, 0)
        else:
            lax.fori_loop(g * GROUP, (g + 1) * GROUP, answer, 0)

    project_down(0, True)
    project_down(1, False)
    project_up(0, True)

    def advance(g, _):
        project_down(g, False)
        project_up(g - 1, False)
        return 0

    lax.fori_loop(2, GROUPS, advance, 0)
    project_up(GROUPS - 1, False)

    for load in loads[3:]:
        load.wait()
    to_blocks(base_in, base_blocks)

    tail = returned.at[pl.ds(PER, (POOL - 1) * PER)]
    pltpu.make_async_copy(tail, tail, answer_recv).wait()

    kv = 2
    old = ctx * kv
    cols = old + STEPS * BLOCK
    near = BLOCK // kv
    shape = (STEPS * heads, cols)
    col = lax.broadcasted_iota(jnp.int32, shape, 1)
    query_row = lax.broadcasted_iota(jnp.int32, shape, 0)
    same_head = (query_row % heads) // (heads // kv) == col % kv
    fresh = col - old
    is_old = col < old
    reachable = fresh // BLOCK <= query_row // heads
    old_key = jnp.where(same_head & is_old, col, 1 << 20)
    fresh_key = jnp.where(same_head & ~is_old & reachable, (fresh % BLOCK) // kv, -1)
    inv = 1.0 / (LANES**0.5)
    per_row = ctx // page

    def one_row(r, tile, within):
        answer_at = row_answer[r]
        queries = []
        for s in range(STEPS):
            at = pl.multiple_of((s * rows + r) * BLOCK, BLOCK)
            delta = returned[answer_at + s * SLOTS].astype(f32)
            queries.append((base_blocks[pl.ds(at, BLOCK), :] + delta).astype(bf16))
        query = jnp.concatenate(queries, axis=0)
        ids = [pages[r * per_row + i] for i in range(per_row)]
        fresh_at = [
            pl.ds(pl.multiple_of(s * rows * kv + tile * BLOCK, BLOCK), BLOCK)
            for s in range(STEPS)
        ]
        key = jnp.concatenate(
            [keys[i] for i in ids] + [new_keys[at, :] for at in fresh_at], axis=0
        )
        value = jnp.concatenate(
            [values[i] for i in ids] + [new_values[at, :] for at in fresh_at], axis=0
        )
        scores = (
            lax.dot_general(query, key, (((1,), (1,)), ((), ())), preferred_element_type=f32) * inv
        )
        live = (old_key < lengths[r] * kv) | (fresh_key == within)
        scores = jnp.where(live, scores, -1e30)
        top = jnp.max(scores, axis=-1, keepdims=True)
        e = jnp.exp(scores - top)
        weights = (e / jnp.sum(e, axis=-1, keepdims=True)).astype(bf16)
        result = jnp.dot(weights, value, preferred_element_type=f32)
        for s in range(STEPS):
            at = pl.multiple_of((s * rows + r) * BLOCK, BLOCK)
            out_blocks[pl.ds(at, BLOCK), :] = result[s * heads : (s + 1) * heads]

    def eight_rows(tile, _):
        for within in range(near):
            one_row(tile * near + within, tile, within)
        return 0

    lax.fori_loop(0, rows // near, eight_rows, 0)

    for s in range(STEPS):
        for c in range(BLOCK):
            out_ref[s, :, c * LANES : (c + 1) * LANES] = out_blocks[
                pl.ds(s * rows * BLOCK + c, rows, stride=BLOCK), :
            ].astype(bf16)

    others = sent.at[pl.ds(PER, (POOL - 1) * PER)]
    pltpu.make_async_copy(others, others, x_send).wait()
    others = answers.at[pl.ds(PER, (POOL - 1) * PER)]
    pltpu.make_async_copy(others, others, answer_send).wait()
    others = got_picks.at[pl.ds(1, POOL - 1)]
    pltpu.make_async_copy(others, others, pick_send).wait()
    pltpu.make_async_copy(parts, parts, part_send).wait()


def shards(
    normed_input,
    base_query_output,
    adapter_down_weight,
    adapter_up_weight,
    row_adapter_index,
    paged_key_cache,
    paged_value_cache,
    step_token_keys,
    step_token_values,
    row_page_table,
    lengths,
):
    rows = row_adapter_index.shape[0]
    features = normed_input.shape[2]
    held, rank = adapter_up_weight.shape[:2]
    count, page, kv, head = paged_key_cache.shape
    ctx = page * row_page_table.shape[1]
    me = lax.axis_index("pool")

    owner = row_adapter_index // held
    local = row_adapter_index % held
    order = jnp.arange(rows, dtype=jnp.int32)
    earlier = jnp.sum(
        ((owner[None, :] == owner[:, None]) & (order[None, :] < order[:, None])).astype(jnp.int32),
        axis=1,
    )
    row_slot = position(me, owner) * SLOTS + earlier
    place = jnp.arange(POOL * SLOTS, dtype=jnp.int32)[:, None] == row_slot[None, :]
    slot_row = jnp.sum(jnp.where(place, order[None, :], 0), axis=1)
    lane = jnp.arange(LANES, dtype=jnp.int32)
    wanted = (row_slot[:, None] % SLOTS) * held + local[:, None] == lane[None, :]
    toward = jnp.arange(POOL, dtype=jnp.int32)[:, None] == row_slot[None, :] // SLOTS
    picks = jnp.sum(
        (toward[:, :, None] & wanted[None, :, :]).astype(jnp.float32), axis=1
    ).reshape(POOL, 1, LANES)

    bf16, f32 = jnp.bfloat16, jnp.float32
    smem = pl.BlockSpec(memory_space=pltpu.SMEM)
    vmem = pl.BlockSpec(memory_space=pltpu.VMEM)
    anywhere = pl.BlockSpec(memory_space=pl.ANY)
    dma = pltpu.SemaphoreType.DMA
    grows = GROUP * PER
    width = held * rank
    return pl.pallas_call(
        functools.partial(kernel, rows, ctx, page),
        out_shape=jax.ShapeDtypeStruct((STEPS, rows, features), bf16),
        in_specs=[smem] * 4 + [vmem] + [anywhere] * 8,
        out_specs=vmem,
        scratch_shapes=[
            pltpu.VMEM((STEPS, rows, features), bf16),
            pltpu.VMEM((STEPS, rows, features), bf16),
            pltpu.VMEM((width, features), bf16),
            pltpu.VMEM((width, features), bf16),
            pltpu.VMEM((count, page * kv, head), bf16),
            pltpu.VMEM((count, page * kv, head), bf16),
            pltpu.VMEM((STEPS * rows * kv, head), bf16),
            pltpu.VMEM((STEPS * rows * kv, head), bf16),
            pltpu.VMEM((STEPS * rows, BLOCK, LANES), bf16),
            pltpu.VMEM((STEPS * rows * BLOCK, LANES), f32),
            pltpu.VMEM((STEPS * rows * BLOCK, LANES), f32),
            pltpu.VMEM((POOL * PER, BLOCK, LANES), bf16),
            pltpu.VMEM((POOL * PER, BLOCK, LANES), bf16),
            pltpu.VMEM((POOL, 1, LANES), f32),
            pltpu.VMEM((GROUPS, grows, width), bf16),
            pltpu.VMEM((GROUPS, grows, LANES), f32),
            pltpu.VMEM((GROUPS, TP - 1, grows, LANES), f32),
            pltpu.VMEM((grows * BLOCK, LANES), f32),
            pltpu.VMEM((POOL * PER, BLOCK, LANES), bf16),
            pltpu.VMEM((POOL * PER, BLOCK, LANES), bf16),
            dma((8,)),
            dma,
            dma((GROUPS,)),
            dma,
            dma((GROUPS,)),
            dma,
            dma((GROUPS,)),
            dma,
            dma,
        ],
        compiler_params=pltpu.CompilerParams(
            collective_id=0, has_side_effects=True, vmem_limit_bytes=60 << 20
        ),
        cost_estimate=pl.CostEstimate(
            flops=3_000_000_000, bytes_accessed=12_000_000, transcendentals=1_000_000
        ),
        name="adapters_and_attention",
    )(
        slot_row,
        row_slot // SLOTS * PER + row_slot % SLOTS,
        row_page_table.reshape(-1),
        lengths,
        picks,
        normed_input,
        base_query_output,
        adapter_down_weight.transpose(1, 2, 0).reshape(width, features),
        adapter_up_weight.reshape(width, features),
        paged_key_cache.reshape(count, page * kv, head),
        paged_value_cache.reshape(count, page * kv, head),
        step_token_keys.reshape(STEPS * rows * kv, head),
        step_token_values.reshape(STEPS * rows * kv, head),
    )


def solution(mesh):
    placed = (
        P(None, "pool", "tp"),
        P(None, "pool", "tp"),
        P("tp", "pool", None),
        P("pool", None, "tp"),
        P("pool"),
        P("pool", None, "tp", None),
        P("pool", None, "tp", None),
        P(None, "pool", "tp", None),
        P(None, "pool", "tp", None),
        P("pool", None),
        P("pool"),
    )
    return jax.shard_map(
        shards, mesh=mesh, in_specs=placed, out_specs=P(None, "pool", "tp"), check_vma=False
    )
```

```python
import functools

import jax
import jax.numpy as jnp
from jax import lax
from jax.experimental import pallas as pl
from jax.experimental.pallas import tpu as pltpu
from jax.sharding import PartitionSpec as P

ADAPTER_SCALE = 0.5
LOG2_E = 1.4426950408889634
MESH = pl.DeviceIdType.MESH
Y, Z, C = 4, 8, 2
POOL = Y * Z * C
TP = 4
GROUP = 8
GROUPS = POOL // GROUP
STEPS = 2
SLOTS = 2
PER = STEPS * SLOTS
BLOCK = 16
LANES = 128


def offsets(k):
    return k // (Z * C), k % Z, (k // Z) % C


def ahead(me, k):
    dy, dz, dc = offsets(k)
    y, z, c = me // (Z * C), (me // C) % Z, me % C
    return (((y + dy) % Y) * Z + (z + dz) % Z) * C + (c + dc) % C


def behind(me, k):
    dy, dz, dc = offsets(k)
    y, z, c = me // (Z * C), (me // C) % Z, me % C
    return (((y + Y - dy) % Y) * Z + (z + Z - dz) % Z) * C + (c + C - dc) % C


def position(me, other):
    y, z, c = me // (Z * C), (me // C) % Z, me % C
    oy, oz, oc = other // (Z * C), (other // C) % Z, other % C
    dy, dz, dc = (oy - y + Y) % Y, (oz - z + Z) % Z, (oc - c + C) % C
    return (dy * C + dc) * Z + dz


def kernel(
    rows,
    ctx,
    page,
    slot_row,
    row_answer,
    pages,
    lengths,
    picks,
    x_hbm,
    base_hbm,
    down_hbm,
    up_hbm,
    key_hbm,
    value_hbm,
    new_key_hbm,
    new_value_hbm,
    out_ref,
    x_in,
    base_in,
    down,
    up,
    keys,
    values,
    new_keys,
    new_values,
    x_blocks,
    base_blocks,
    out_blocks,
    sent,
    got,
    got_picks,
    masks,
    own_part,
    parts,
    wide,
    answers,
    returned,
    local_sems,
    x_send,
    x_recv,
    pick_send,
    pick_recv,
    part_send,
    part_recv,
    answer_send,
    answer_recv,
):
    me = lax.axis_index("pool")
    my_tp = lax.axis_index("tp")
    heads = BLOCK
    f32, bf16 = jnp.float32, jnp.bfloat16

    barrier = pltpu.get_barrier_semaphore()

    def greet(k, _):
        pl.semaphore_signal(
            barrier, inc=1, device_id={"pool": ahead(me, k)}, device_id_type=MESH
        )
        return 0

    lax.fori_loop(1, POOL, greet, 0)
    for t in range(1, TP):
        pl.semaphore_signal(
            barrier, inc=1, device_id={"tp": (my_tp + t) % TP}, device_id_type=MESH
        )

    loads = [
        pltpu.make_async_copy(src, dst, local_sems.at[i])
        for i, (src, dst) in enumerate(
            (
                (x_hbm, x_in),
                (down_hbm, down),
                (up_hbm, up),
                (base_hbm, base_in),
                (key_hbm, keys),
                (value_hbm, values),
                (new_key_hbm, new_keys),
                (new_value_hbm, new_values),
            )
        )
    ]
    for load in loads:
        load.start()

    def to_blocks(src, dst):
        for s in range(STEPS):
            for c in range(BLOCK):
                dst[pl.ds(s * rows * BLOCK + c, rows, stride=BLOCK), :] = src[
                    s, :, c * LANES : (c + 1) * LANES
                ].astype(f32)

    loads[0].wait()
    to_blocks(x_in, base_blocks)
    x_blocks[...] = base_blocks[...].astype(bf16).reshape(STEPS * rows, BLOCK, LANES)

    pl.semaphore_wait(barrier, POOL - 1 + TP - 1)

    def message(k, src, dst, send_sem, recv_sem, to):
        return pltpu.make_async_remote_copy(
            src_ref=src.at[pl.ds(k * PER, PER)],
            dst_ref=dst.at[pl.ds(k * PER, PER)],
            send_sem=send_sem,
            recv_sem=recv_sem,
            device_id={"pool": to},
            device_id_type=MESH,
        )

    def blocks_of(k, dst):
        for j in range(SLOTS):
            row = slot_row[k * SLOTS + j]
            for s in range(STEPS):
                dst[k * PER + s * SLOTS + j] = x_blocks[row + s * rows]

    def send_row(k, _):
        blocks_of(k, sent)
        to = ahead(me, k)
        pltpu.make_async_remote_copy(
            src_ref=picks.at[k],
            dst_ref=got_picks.at[k],
            send_sem=pick_send,
            recv_sem=pick_recv.at[k // GROUP],
            device_id={"pool": to},
            device_id_type=MESH,
        ).start()
        message(k, sent, got, x_send, x_recv.at[k // GROUP], to).start()
        return 0

    lax.fori_loop(1, POOL, send_row, 0)
    blocks_of(0, got)
    got_picks[0] = picks[0]

    loads[1].wait()
    loads[2].wait()

    grows = GROUP * PER
    width = down.shape[0]
    rank = width // 8
    spread = (
        lax.broadcasted_iota(jnp.int32, (grows, GROUP), 0) // PER
        == lax.broadcasted_iota(jnp.int32, (grows, GROUP), 1)
    ).astype(f32)
    lane = lax.broadcasted_iota(jnp.int32, (grows, LANES), 1)
    slot = lax.broadcasted_iota(jnp.int32, (grows, LANES), 0) % SLOTS
    slot_lanes = (lane // 8 == slot).astype(f32)
    widen = (
        lax.broadcasted_iota(jnp.int32, (LANES, width), 0) % 8
        == lax.broadcasted_iota(jnp.int32, (LANES, width), 1) // rank
    ).astype(f32)

    def group_bytes(g, first, ref, per, sem):
        lo, n = g * GROUP * per, GROUP * per
        if first:
            lo, n = per, (GROUP - 1) * per
        part = ref.at[pl.ds(lo, n)]
        pltpu.make_async_copy(part, part, sem).wait()

    def project_down(g, first):
        group_bytes(g, first, got, PER, x_recv.at[g])
        group_bytes(g, first, got_picks, 1, pick_recv.at[g])
        wide[...] = got[pl.ds(g * grows, grows)].reshape(grows * BLOCK, LANES).astype(f32)
        features = jnp.concatenate(
            [wide[pl.ds(c, grows, stride=BLOCK), :] for c in range(BLOCK)], axis=1
        ).astype(bf16)
        product = lax.dot_general(
            features, down[...], (((1,), (1,)), ((), ())), preferred_element_type=f32
        )
        chosen = got_picks[pl.ds(g * GROUP, GROUP)].reshape(GROUP, LANES)
        chosen = jnp.dot(spread, chosen, preferred_element_type=f32) * slot_lanes
        mask = jnp.dot(chosen, widen, preferred_element_type=f32)
        masks[g] = mask.astype(bf16)
        product = product * mask
        part = product[:, :LANES]
        for i in range(1, width // LANES):
            part = part + product[:, i * LANES : (i + 1) * LANES]
        own_part[g] = part
        for t in range(1, TP):
            pltpu.make_async_remote_copy(
                src_ref=own_part.at[g],
                dst_ref=parts.at[g, t - 1],
                send_sem=part_send,
                recv_sem=part_recv.at[g],
                device_id={"tp": (my_tp + t) % TP},
                device_id_type=MESH,
            ).start()

    def project_up(g, first):
        pltpu.make_async_copy(parts.at[g], parts.at[g], part_recv.at[g]).wait()
        u = own_part[g] + parts[g, 0] + parts[g, 1] + parts[g, 2]
        u = u.astype(bf16)
        u = jnp.concatenate([u] * (width // LANES), axis=1) * masks[g]
        delta = jnp.dot(u, up[...], preferred_element_type=f32) * ADAPTER_SCALE
        for c in range(BLOCK):
            wide[pl.ds(c, grows, stride=BLOCK), :] = delta[:, c * LANES : (c + 1) * LANES]
        answers[pl.ds(g * grows, grows)] = (
            wide[...].astype(bf16).reshape(grows, BLOCK, LANES)
        )

        def answer(k, _):
            message(k, answers, returned, answer_send, answer_recv, behind(me, k)).start()
            return 0

        if first:
            returned[pl.ds(0, PER)] = answers[pl.ds(0, PER)]
            lax.fori_loop(1, GROUP, answer, 0)
        else:
            lax.fori_loop(g * GROUP, (g + 1) * GROUP, answer, 0)

    project_down(0, True)
    project_down(1, False)
    project_up(0, True)

    def advance(g, _):
        project_down(g, False)
        project_up(g - 1, False)
        return 0

    lax.fori_loop(2, GROUPS, advance, 0)
    project_up(GROUPS - 1, False)

    for load in loads[3:]:
        load.wait()
    to_blocks(base_in, base_blocks)

    tail = returned.at[pl.ds(PER, (POOL - 1) * PER)]
    pltpu.make_async_copy(tail, tail, answer_recv).wait()

    kv = 2
    old = ctx * kv
    near = BLOCK // kv
    mine = STEPS * heads
    col = lax.broadcasted_iota(jnp.int32, (mine, old), 1)
    query_row = lax.broadcasted_iota(jnp.int32, (mine, old), 0)
    old_key = jnp.where((query_row % heads) // (heads // kv) == col % kv, col, 1 << 20)
    shape = (near * mine, STEPS * BLOCK)
    col = lax.broadcasted_iota(jnp.int32, shape, 1)
    query_row = lax.broadcasted_iota(jnp.int32, shape, 0)
    fresh_live = (
        ((col % BLOCK) // kv == query_row // mine)
        & (col // BLOCK <= (query_row % mine) // heads)
        & (col % kv == (query_row % heads) // (heads // kv))
    )
    per_row = ctx // page
    scale = LOG2_E / (LANES**0.5)

    def eight_rows(tile, _):
        queries = []
        for i in range(near):
            r = tile * near + i
            for s in range(STEPS):
                at = pl.multiple_of((s * rows + r) * BLOCK, BLOCK)
                delta = returned[row_answer[r] + s * SLOTS].astype(f32)
                queries.append((base_blocks[pl.ds(at, BLOCK), :] + delta).astype(bf16))
        query = jnp.concatenate(queries, axis=0)
        fresh_at = [
            pl.ds(pl.multiple_of(s * rows * kv + tile * BLOCK, BLOCK), BLOCK)
            for s in range(STEPS)
        ]
        new_key = jnp.concatenate([new_keys[at, :] for at in fresh_at], axis=0)
        new_value = jnp.concatenate([new_values[at, :] for at in fresh_at], axis=0)
        transposed = (((1,), (1,)), ((), ()))
        fresh = lax.dot_general(query, new_key, transposed, preferred_element_type=f32)
        fresh = jnp.where(fresh_live, fresh, -1e30)
        scores = []
        for i in range(near):
            r = tile * near + i
            key = jnp.concatenate([keys[pages[p, r]] for p in range(per_row)], axis=0)
            part = lax.dot_general(
                query[i * mine : (i + 1) * mine], key, transposed, preferred_element_type=f32
            )
            scores.append(jnp.where(old_key < lengths[r] * kv, part, -1e30))
        scores = jnp.concatenate(scores, axis=0)
        top = jnp.maximum(
            jnp.max(scores, axis=-1, keepdims=True), jnp.max(fresh, axis=-1, keepdims=True)
        )
        e_old = jnp.exp2((scores - top) * scale)
        e_new = jnp.exp2((fresh - top) * scale)
        total = jnp.sum(e_old, axis=-1, keepdims=True) + jnp.sum(e_new, axis=-1, keepdims=True)
        share = 1.0 / total
        w_old = (e_old * share).astype(bf16)
        w_new = (e_new * share).astype(bf16)
        result = jnp.dot(w_new, new_value, preferred_element_type=f32)
        for i in range(near):
            r = tile * near + i
            value = jnp.concatenate([values[pages[p, r]] for p in range(per_row)], axis=0)
            both = result[i * mine : (i + 1) * mine] + jnp.dot(
                w_old[i * mine : (i + 1) * mine], value, preferred_element_type=f32
            )
            for s in range(STEPS):
                at = pl.multiple_of((s * rows + r) * BLOCK, BLOCK)
                out_blocks[pl.ds(at, BLOCK), :] = both[s * heads : (s + 1) * heads]
        return 0

    lax.fori_loop(0, rows // near, eight_rows, 0)

    for s in range(STEPS):
        for c in range(BLOCK):
            out_ref[s, :, c * LANES : (c + 1) * LANES] = out_blocks[
                pl.ds(s * rows * BLOCK + c, rows, stride=BLOCK), :
            ].astype(bf16)

    others = sent.at[pl.ds(PER, (POOL - 1) * PER)]
    pltpu.make_async_copy(others, others, x_send).wait()
    others = answers.at[pl.ds(PER, (POOL - 1) * PER)]
    pltpu.make_async_copy(others, others, answer_send).wait()
    others = got_picks.at[pl.ds(1, POOL - 1)]
    pltpu.make_async_copy(others, others, pick_send).wait()
    pltpu.make_async_copy(parts, parts, part_send).wait()


def shards(
    normed_input,
    base_query_output,
    adapter_down_weight,
    adapter_up_weight,
    row_adapter_index,
    paged_key_cache,
    paged_value_cache,
    step_token_keys,
    step_token_values,
    row_page_table,
    lengths,
):
    rows = row_adapter_index.shape[0]
    features = normed_input.shape[2]
    held, rank = adapter_up_weight.shape[:2]
    count, page, kv, head = paged_key_cache.shape
    ctx = page * row_page_table.shape[1]
    me = lax.axis_index("pool")

    owner = row_adapter_index // held
    local = row_adapter_index % held
    order = jnp.arange(rows, dtype=jnp.int32)
    earlier = jnp.sum(
        ((owner[None, :] == owner[:, None]) & (order[None, :] < order[:, None])).astype(jnp.int32),
        axis=1,
    )
    row_slot = position(me, owner) * SLOTS + earlier
    place = jnp.arange(POOL * SLOTS, dtype=jnp.int32)[:, None] == row_slot[None, :]
    slot_row = jnp.sum(jnp.where(place, order[None, :], 0), axis=1)
    lane = jnp.arange(LANES, dtype=jnp.int32)
    wanted = (row_slot[:, None] % SLOTS) * held + local[:, None] == lane[None, :]
    toward = jnp.arange(POOL, dtype=jnp.int32)[:, None] == row_slot[None, :] // SLOTS
    picks = jnp.sum(
        (toward[:, :, None] & wanted[None, :, :]).astype(jnp.float32), axis=1
    ).reshape(POOL, 1, LANES)

    bf16, f32 = jnp.bfloat16, jnp.float32
    smem = pl.BlockSpec(memory_space=pltpu.SMEM)
    vmem = pl.BlockSpec(memory_space=pltpu.VMEM)
    anywhere = pl.BlockSpec(memory_space=pl.ANY)
    dma = pltpu.SemaphoreType.DMA
    grows = GROUP * PER
    width = held * rank
    return pl.pallas_call(
        functools.partial(kernel, rows, ctx, page),
        out_shape=jax.ShapeDtypeStruct((STEPS, rows, features), bf16),
        in_specs=[smem] * 4 + [vmem] + [anywhere] * 8,
        out_specs=vmem,
        scratch_shapes=[
            pltpu.VMEM((STEPS, rows, features), bf16),
            pltpu.VMEM((STEPS, rows, features), bf16),
            pltpu.VMEM((width, features), bf16),
            pltpu.VMEM((width, features), bf16),
            pltpu.VMEM((count, page * kv, head), bf16),
            pltpu.VMEM((count, page * kv, head), bf16),
            pltpu.VMEM((STEPS * rows * kv, head), bf16),
            pltpu.VMEM((STEPS * rows * kv, head), bf16),
            pltpu.VMEM((STEPS * rows, BLOCK, LANES), bf16),
            pltpu.VMEM((STEPS * rows * BLOCK, LANES), f32),
            pltpu.VMEM((STEPS * rows * BLOCK, LANES), f32),
            pltpu.VMEM((POOL * PER, BLOCK, LANES), bf16),
            pltpu.VMEM((POOL * PER, BLOCK, LANES), bf16),
            pltpu.VMEM((POOL, 1, LANES), f32),
            pltpu.VMEM((GROUPS, grows, width), bf16),
            pltpu.VMEM((GROUPS, grows, LANES), f32),
            pltpu.VMEM((GROUPS, TP - 1, grows, LANES), f32),
            pltpu.VMEM((grows * BLOCK, LANES), f32),
            pltpu.VMEM((POOL * PER, BLOCK, LANES), bf16),
            pltpu.VMEM((POOL * PER, BLOCK, LANES), bf16),
            dma((8,)),
            dma,
            dma((GROUPS,)),
            dma,
            dma((GROUPS,)),
            dma,
            dma((GROUPS,)),
            dma,
            dma,
        ],
        compiler_params=pltpu.CompilerParams(
            collective_id=0, has_side_effects=True, vmem_limit_bytes=60 << 20
        ),
        cost_estimate=pl.CostEstimate(
            flops=3_000_000_000, bytes_accessed=12_000_000, transcendentals=1_000_000
        ),
        name="adapters_and_attention",
    )(
        slot_row,
        row_slot // SLOTS * PER + row_slot % SLOTS,
        row_page_table.T,
        lengths,
        picks,
        normed_input,
        base_query_output,
        adapter_down_weight.transpose(1, 2, 0).reshape(width, features),
        adapter_up_weight.reshape(width, features),
        paged_key_cache.reshape(count, page * kv, head),
        paged_value_cache.reshape(count, page * kv, head),
        step_token_keys.reshape(STEPS * rows * kv, head),
        step_token_values.reshape(STEPS * rows * kv, head),
    )


def solution(mesh):
    placed = (
        P(None, "pool", "tp"),
        P(None, "pool", "tp"),
        P("tp", "pool", None),
        P("pool", None, "tp"),
        P("pool"),
        P("pool", None, "tp", None),
        P("pool", None, "tp", None),
        P(None, "pool", "tp", None),
        P(None, "pool", "tp", None),
        P("pool", None),
        P("pool"),
    )
    return jax.shard_map(
        shards, mesh=mesh, in_specs=placed, out_specs=P(None, "pool", "tp"), check_vma=False
    )
```

```python
import functools

import jax
import jax.numpy as jnp
from jax import lax
from jax.experimental import pallas as pl
from jax.experimental.pallas import tpu as pltpu
from jax.sharding import PartitionSpec as P

ADAPTER_SCALE = 0.5
LOG2_E = 1.4426950408889634
MESH = pl.DeviceIdType.MESH
Y, Z, C = 4, 8, 2
POOL = Y * Z * C
TP = 4
GROUP = 8
GROUPS = POOL // GROUP
BATCH = 16
BATCHES = POOL // BATCH
THREE = 3
STEPS = 2
SLOTS = 2
PER = STEPS * SLOTS
BLOCK = 16
LANES = 128


def offsets(k):
    return k // (Z * C), k % Z, (k // Z) % C


def ahead(me, k):
    dy, dz, dc = offsets(k)
    y, z, c = me // (Z * C), (me // C) % Z, me % C
    return (((y + dy) % Y) * Z + (z + dz) % Z) * C + (c + dc) % C


def behind(me, k):
    dy, dz, dc = offsets(k)
    y, z, c = me // (Z * C), (me // C) % Z, me % C
    return (((y + Y - dy) % Y) * Z + (z + Z - dz) % Z) * C + (c + C - dc) % C


def position(me, other):
    y, z, c = me // (Z * C), (me // C) % Z, me % C
    oy, oz, oc = other // (Z * C), (other // C) % Z, other % C
    dy, dz, dc = (oy - y + Y) % Y, (oz - z + Z) % Z, (oc - c + C) % C
    return (dy * C + dc) * Z + dz


def greet_all(me, my_tp):
    barrier = pltpu.get_barrier_semaphore()

    def greet(k, _):
        pl.semaphore_signal(
            barrier, inc=1, device_id={"pool": ahead(me, k)}, device_id_type=MESH
        )
        return 0

    lax.fori_loop(1, POOL, greet, 0)
    for t in range(1, TP):
        pl.semaphore_signal(
            barrier, inc=1, device_id={"tp": (my_tp + t) % TP}, device_id_type=MESH
        )
    return barrier


def start_loads(pairs, sems):
    loads = [pltpu.make_async_copy(src, dst, sems.at[i]) for i, (src, dst) in enumerate(pairs)]
    for load in loads:
        load.start()
    return loads


def to_blocks(rows, src, dst):
    for s in range(STEPS):
        for c in range(BLOCK):
            dst[pl.ds(s * rows * BLOCK + c, rows, stride=BLOCK), :] = src[
                s, :, c * LANES : (c + 1) * LANES
            ].astype(jnp.float32)


def await_bytes(ref, sem):
    pltpu.make_async_copy(ref, ref, sem).wait()


def attend(
    rows,
    ctx,
    page,
    row_answer,
    pages,
    lengths,
    keys,
    values,
    new_keys,
    new_values,
    base_blocks,
    returned,
    out_blocks,
    out_ref,
):
    heads = BLOCK
    f32, bf16 = jnp.float32, jnp.bfloat16
    kv = 2
    old = ctx * kv
    near = BLOCK // kv
    mine = STEPS * heads
    col = lax.broadcasted_iota(jnp.int32, (mine, old), 1)
    query_row = lax.broadcasted_iota(jnp.int32, (mine, old), 0)
    old_key = jnp.where((query_row % heads) // (heads // kv) == col % kv, col, 1 << 20)
    shape = (near * mine, STEPS * BLOCK)
    col = lax.broadcasted_iota(jnp.int32, shape, 1)
    query_row = lax.broadcasted_iota(jnp.int32, shape, 0)
    fresh_live = (
        ((col % BLOCK) // kv == query_row // mine)
        & (col // BLOCK <= (query_row % mine) // heads)
        & (col % kv == (query_row % heads) // (heads // kv))
    )
    per_row = ctx // page
    scale = LOG2_E / (LANES**0.5)

    def eight_rows(tile, _):
        queries = []
        for i in range(near):
            r = tile * near + i
            for s in range(STEPS):
                at = pl.multiple_of((s * rows + r) * BLOCK, BLOCK)
                delta = returned[row_answer[s, r]].astype(f32)
                queries.append((base_blocks[pl.ds(at, BLOCK), :] + delta).astype(bf16))
        query = jnp.concatenate(queries, axis=0)
        fresh_at = [
            pl.ds(pl.multiple_of(s * rows * kv + tile * BLOCK, BLOCK), BLOCK)
            for s in range(STEPS)
        ]
        new_key = jnp.concatenate([new_keys[at, :] for at in fresh_at], axis=0)
        new_value = jnp.concatenate([new_values[at, :] for at in fresh_at], axis=0)
        transposed = (((1,), (1,)), ((), ()))
        fresh = lax.dot_general(query, new_key, transposed, preferred_element_type=f32)
        fresh = jnp.where(fresh_live, fresh, -1e30)
        scores = []
        for i in range(near):
            r = tile * near + i
            key = jnp.concatenate([keys[pages[p, r]] for p in range(per_row)], axis=0)
            part = lax.dot_general(
                query[i * mine : (i + 1) * mine], key, transposed, preferred_element_type=f32
            )
            scores.append(jnp.where(old_key < lengths[r] * kv, part, -1e30))
        scores = jnp.concatenate(scores, axis=0)
        top = jnp.maximum(
            jnp.max(scores, axis=-1, keepdims=True), jnp.max(fresh, axis=-1, keepdims=True)
        )
        e_old = jnp.exp2((scores - top) * scale)
        e_new = jnp.exp2((fresh - top) * scale)
        total = jnp.sum(e_old, axis=-1, keepdims=True) + jnp.sum(e_new, axis=-1, keepdims=True)
        share = 1.0 / total
        w_old = (e_old * share).astype(bf16)
        w_new = (e_new * share).astype(bf16)
        result = jnp.dot(w_new, new_value, preferred_element_type=f32)
        for i in range(near):
            r = tile * near + i
            value = jnp.concatenate([values[pages[p, r]] for p in range(per_row)], axis=0)
            both = result[i * mine : (i + 1) * mine] + jnp.dot(
                w_old[i * mine : (i + 1) * mine], value, preferred_element_type=f32
            )
            for s in range(STEPS):
                at = pl.multiple_of((s * rows + r) * BLOCK, BLOCK)
                out_blocks[pl.ds(at, BLOCK), :] = both[s * heads : (s + 1) * heads]
        return 0

    lax.fori_loop(0, rows // near, eight_rows, 0)

    for s in range(STEPS):
        for c in range(BLOCK):
            out_ref[s, :, c * LANES : (c + 1) * LANES] = out_blocks[
                pl.ds(s * rows * BLOCK + c, rows, stride=BLOCK), :
            ].astype(bf16)


def every_slot_kernel(
    rows,
    ctx,
    page,
    slot_row,
    row_answer,
    pages,
    lengths,
    picks,
    x_hbm,
    base_hbm,
    down_hbm,
    up_hbm,
    key_hbm,
    value_hbm,
    new_key_hbm,
    new_value_hbm,
    out_ref,
    x_in,
    base_in,
    down,
    up,
    keys,
    values,
    new_keys,
    new_values,
    x_blocks,
    base_blocks,
    out_blocks,
    sent,
    got,
    got_picks,
    masks,
    own_part,
    parts,
    wide,
    answers,
    returned,
    local_sems,
    x_send,
    x_recv,
    pick_send,
    pick_recv,
    part_send,
    part_recv,
    answer_send,
    answer_recv,
):
    me = lax.axis_index("pool")
    my_tp = lax.axis_index("tp")
    f32, bf16 = jnp.float32, jnp.bfloat16

    barrier = greet_all(me, my_tp)
    loads = start_loads(
        (
            (x_hbm, x_in),
            (down_hbm, down),
            (up_hbm, up),
            (base_hbm, base_in),
            (key_hbm, keys),
            (value_hbm, values),
            (new_key_hbm, new_keys),
            (new_value_hbm, new_values),
        ),
        local_sems,
    )
    loads[0].wait()
    to_blocks(rows, x_in, base_blocks)
    x_blocks[...] = base_blocks[...].astype(bf16).reshape(STEPS * rows, BLOCK, LANES)

    pl.semaphore_wait(barrier, POOL - 1 + TP - 1)

    def message(k, src, dst, send_sem, recv_sem, to):
        return pltpu.make_async_remote_copy(
            src_ref=src.at[pl.ds(k * PER, PER)],
            dst_ref=dst.at[pl.ds(k * PER, PER)],
            send_sem=send_sem,
            recv_sem=recv_sem,
            device_id={"pool": to},
            device_id_type=MESH,
        )

    def blocks_of(k, dst):
        for j in range(SLOTS):
            row = slot_row[k * SLOTS + j]
            for s in range(STEPS):
                dst[k * PER + s * SLOTS + j] = x_blocks[row + s * rows]

    def send_row(k, _):
        blocks_of(k, sent)
        to = ahead(me, k)
        pltpu.make_async_remote_copy(
            src_ref=picks.at[k],
            dst_ref=got_picks.at[k],
            send_sem=pick_send,
            recv_sem=pick_recv.at[k // GROUP],
            device_id={"pool": to},
            device_id_type=MESH,
        ).start()
        message(k, sent, got, x_send, x_recv.at[k // GROUP], to).start()
        return 0

    lax.fori_loop(1, POOL, send_row, 0)
    blocks_of(0, got)
    got_picks[0] = picks[0]

    loads[1].wait()
    loads[2].wait()

    grows = GROUP * PER
    width = down.shape[0]
    rank = width // 8
    spread = (
        lax.broadcasted_iota(jnp.int32, (grows, GROUP), 0) // PER
        == lax.broadcasted_iota(jnp.int32, (grows, GROUP), 1)
    ).astype(f32)
    lane = lax.broadcasted_iota(jnp.int32, (grows, LANES), 1)
    slot = lax.broadcasted_iota(jnp.int32, (grows, LANES), 0) % SLOTS
    slot_lanes = (lane // 8 == slot).astype(f32)
    widen = (
        lax.broadcasted_iota(jnp.int32, (LANES, width), 0) % 8
        == lax.broadcasted_iota(jnp.int32, (LANES, width), 1) // rank
    ).astype(f32)

    def group_bytes(g, first, ref, per, sem):
        lo, n = g * GROUP * per, GROUP * per
        if first:
            lo, n = per, (GROUP - 1) * per
        part = ref.at[pl.ds(lo, n)]
        pltpu.make_async_copy(part, part, sem).wait()

    def project_down(g, first):
        group_bytes(g, first, got, PER, x_recv.at[g])
        group_bytes(g, first, got_picks, 1, pick_recv.at[g])
        wide[...] = got[pl.ds(g * grows, grows)].reshape(grows * BLOCK, LANES).astype(f32)
        features = jnp.concatenate(
            [wide[pl.ds(c, grows, stride=BLOCK), :] for c in range(BLOCK)], axis=1
        ).astype(bf16)
        product = lax.dot_general(
            features, down[...], (((1,), (1,)), ((), ())), preferred_element_type=f32
        )
        chosen = got_picks[pl.ds(g * GROUP, GROUP)].reshape(GROUP, LANES)
        chosen = jnp.dot(spread, chosen, preferred_element_type=f32) * slot_lanes
        mask = jnp.dot(chosen, widen, preferred_element_type=f32)
        masks[g] = mask.astype(bf16)
        product = product * mask
        part = product[:, :LANES]
        for i in range(1, width // LANES):
            part = part + product[:, i * LANES : (i + 1) * LANES]
        own_part[g] = part
        for t in range(1, TP):
            pltpu.make_async_remote_copy(
                src_ref=own_part.at[g],
                dst_ref=parts.at[g, t - 1],
                send_sem=part_send,
                recv_sem=part_recv.at[g],
                device_id={"tp": (my_tp + t) % TP},
                device_id_type=MESH,
            ).start()

    def project_up(g, first):
        pltpu.make_async_copy(parts.at[g], parts.at[g], part_recv.at[g]).wait()
        u = own_part[g] + parts[g, 0] + parts[g, 1] + parts[g, 2]
        u = u.astype(bf16)
        u = jnp.concatenate([u] * (width // LANES), axis=1) * masks[g]
        delta = jnp.dot(u, up[...], preferred_element_type=f32) * ADAPTER_SCALE
        for c in range(BLOCK):
            wide[pl.ds(c, grows, stride=BLOCK), :] = delta[:, c * LANES : (c + 1) * LANES]
        answers[pl.ds(g * grows, grows)] = (
            wide[...].astype(bf16).reshape(grows, BLOCK, LANES)
        )

        def answer(k, _):
            message(k, answers, returned, answer_send, answer_recv, behind(me, k)).start()
            return 0

        if first:
            returned[pl.ds(0, PER)] = answers[pl.ds(0, PER)]
            lax.fori_loop(1, GROUP, answer, 0)
        else:
            lax.fori_loop(g * GROUP, (g + 1) * GROUP, answer, 0)

    project_down(0, True)
    project_down(1, False)
    project_up(0, True)

    def advance(g, _):
        project_down(g, False)
        project_up(g - 1, False)
        return 0

    lax.fori_loop(2, GROUPS, advance, 0)
    project_up(GROUPS - 1, False)

    for load in loads[3:]:
        load.wait()
    to_blocks(rows, base_in, base_blocks)

    tail = returned.at[pl.ds(PER, (POOL - 1) * PER)]
    pltpu.make_async_copy(tail, tail, answer_recv).wait()

    attend(
        rows,
        ctx,
        page,
        row_answer,
        pages,
        lengths,
        keys,
        values,
        new_keys,
        new_values,
        base_blocks,
        returned,
        out_blocks,
        out_ref,
    )

    others = sent.at[pl.ds(PER, (POOL - 1) * PER)]
    pltpu.make_async_copy(others, others, x_send).wait()
    others = answers.at[pl.ds(PER, (POOL - 1) * PER)]
    pltpu.make_async_copy(others, others, answer_send).wait()
    others = got_picks.at[pl.ds(1, POOL - 1)]
    pltpu.make_async_copy(others, others, pick_send).wait()
    pltpu.make_async_copy(parts, parts, part_send).wait()


def shared_chip_kernel(
    rows,
    ctx,
    page,
    slot_row,
    third_row,
    row_answer,
    pages,
    lengths,
    picks,
    x_hbm,
    base_hbm,
    down_hbm,
    up_hbm,
    key_hbm,
    value_hbm,
    new_key_hbm,
    new_value_hbm,
    out_ref,
    full_ref,
    x_in,
    base_in,
    down,
    up,
    keys,
    values,
    new_keys,
    new_values,
    x_blocks,
    base_blocks,
    out_blocks,
    sent,
    got,
    got_picks,
    masks,
    own_part,
    parts,
    wide,
    answers,
    returned,
    local_sems,
    weight_send,
    weight_recv,
    x_send,
    x_recv,
    pick_send,
    pick_recv,
    part_send,
    part_recv,
    answer_send,
    answer_recv,
):
    me = lax.axis_index("pool")
    my_tp = lax.axis_index("tp")
    my_core = me % C
    f32, bf16 = jnp.float32, jnp.bfloat16
    three = THREE

    barrier = greet_all(me, my_tp)
    width = down_hbm.shape[0]
    my_part = pl.ds(pl.multiple_of(my_core * width, width), width)
    loads = start_loads(
        (
            (x_hbm, x_in),
            (down_hbm, down.at[my_part]),
            (up_hbm, up.at[my_part]),
            (base_hbm, base_in),
            (key_hbm, keys),
            (value_hbm, values),
            (new_key_hbm, new_keys),
            (new_value_hbm, new_values),
        ),
        local_sems,
    )
    loads[0].wait()
    to_blocks(rows, x_in, base_blocks)
    x_blocks[...] = base_blocks[...].astype(bf16).reshape(STEPS * rows, BLOCK, LANES)

    pl.semaphore_wait(barrier, POOL - 1 + TP - 1)

    def push(src, dst, send_sem, recv_sem, to):
        pltpu.make_async_remote_copy(
            src_ref=src,
            dst_ref=dst,
            send_sem=send_sem,
            recv_sem=recv_sem,
            device_id={"pool": to},
            device_id_type=MESH,
        ).start()

    def message(ref, k, n):
        return ref.at[pl.ds(k * n, n)]

    def blocks_of(k, dst):
        row = slot_row[k]
        for s in range(STEPS):
            dst[k * three + s] = x_blocks[row + s * rows]
        dst[k * three + STEPS] = x_blocks[third_row[k] + (ahead(me, k) % C) * rows]

    def send_row(k, _):
        blocks_of(k, sent)
        to, b = ahead(me, k), k // BATCH
        push(message(picks, k, 1), message(got_picks, k, 1), pick_send, pick_recv.at[b], to)
        push(message(sent, k, three), message(got, k, three), x_send, x_recv.at[b], to)
        return 0

    lax.fori_loop(1, BATCH, send_row, 0)
    other = ahead(me, Z)
    push(down_hbm, down.at[my_part], weight_send.at[0], weight_recv.at[0], other)
    lax.fori_loop(BATCH, 2 * BATCH, send_row, 0)
    push(up_hbm, up.at[my_part], weight_send.at[1], weight_recv.at[1], other)
    lax.fori_loop(2 * BATCH, POOL, send_row, 0)
    blocks_of(0, got)
    got_picks[0] = picks[0]

    loads[3].wait()
    to_blocks(rows, base_in, base_blocks)

    held = 8
    rank = width // held
    both = C * held
    brows = BATCH * three
    spread = (
        lax.broadcasted_iota(jnp.int32, (brows, BATCH), 0) // three
        == lax.broadcasted_iota(jnp.int32, (brows, BATCH), 1)
    ).astype(f32)
    slot_lanes = (
        lax.broadcasted_iota(jnp.int32, (brows, LANES), 1) // both
        == (lax.broadcasted_iota(jnp.int32, (brows, LANES), 0) % three) // STEPS
    ).astype(f32)
    widen = (
        lax.broadcasted_iota(jnp.int32, (LANES, C * width), 0) % both
        == lax.broadcasted_iota(jnp.int32, (LANES, C * width), 1) // rank
    ).astype(f32)

    def down_batch(b):
        first = 1 if b == 0 else 0
        await_bytes(got_picks.at[pl.ds(b * BATCH + first, BATCH - first)], pick_recv.at[b])
        chosen = got_picks[pl.ds(b * BATCH, BATCH)].reshape(BATCH, LANES)
        chosen = jnp.dot(spread, chosen, preferred_element_type=f32) * slot_lanes
        mask = jnp.dot(chosen, widen, preferred_element_type=f32)
        masks[b] = mask.astype(bf16)
        await_bytes(
            got.at[pl.ds(b * brows + first * three, brows - first * three)], x_recv.at[b]
        )
        blocks = got[pl.ds(b * brows, brows)]
        wide[...] = blocks.reshape(brows * BLOCK, LANES).astype(f32)
        features = jnp.concatenate(
            [wide[pl.ds(c, brows, stride=BLOCK), :] for c in range(BLOCK)], axis=1
        ).astype(bf16)
        product = lax.dot_general(
            features, down[...], (((1,), (1,)), ((), ())), preferred_element_type=f32
        )
        product = product * mask
        part = product[:, :LANES]
        for i in range(1, C * width // LANES):
            part = part + product[:, i * LANES : (i + 1) * LANES]
        own_part[b] = part
        for t in range(1, TP):
            pltpu.make_async_remote_copy(
                src_ref=own_part.at[b],
                dst_ref=parts.at[b, t - 1],
                send_sem=part_send,
                recv_sem=part_recv.at[b],
                device_id={"tp": (my_tp + t) % TP},
                device_id_type=MESH,
            ).start()

    def up_batch(b):
        await_bytes(parts.at[b], part_recv.at[b])
        u = own_part[b] + parts[b, 0] + parts[b, 1] + parts[b, 2]
        u = jnp.concatenate([u.astype(bf16)] * (C * width // LANES), axis=1) * masks[b]
        delta = jnp.dot(u, up[...], preferred_element_type=f32) * ADAPTER_SCALE
        for c in range(BLOCK):
            wide[pl.ds(c, brows, stride=BLOCK), :] = delta[:, c * LANES : (c + 1) * LANES]
        answers[pl.ds(b * brows, brows)] = wide[...].astype(bf16).reshape(brows, BLOCK, LANES)

        def answer(k, _):
            push(
                message(answers, k, three),
                message(returned, k, three),
                answer_send,
                answer_recv,
                behind(me, k),
            )
            return 0

        if b == 0:
            returned[pl.ds(0, three)] = answers[pl.ds(0, three)]
        lax.fori_loop(max(b * BATCH, 1), (b + 1) * BATCH, answer, 0)

    loads[1].wait()
    await_bytes(down.at[my_part], weight_recv.at[0])
    down_batch(0)
    down_batch(1)
    loads[2].wait()
    await_bytes(up.at[my_part], weight_recv.at[1])
    up_batch(0)
    for b in range(2, BATCHES):
        down_batch(b)
        up_batch(b - 1)
    up_batch(BATCHES - 1)

    full_ref[0, 0] = jnp.max(got_picks[...].reshape(POOL, LANES)[:, 2 * both]).astype(jnp.int32)
    for load in loads[4:]:
        load.wait()
    await_bytes(returned.at[pl.ds(three, (POOL - 1) * three)], answer_recv)
    attend(
        rows,
        ctx,
        page,
        row_answer,
        pages,
        lengths,
        keys,
        values,
        new_keys,
        new_values,
        base_blocks,
        returned,
        out_blocks,
        out_ref,
    )

    await_bytes(down.at[my_part], weight_send.at[0])
    await_bytes(up.at[my_part], weight_send.at[1])
    await_bytes(sent.at[pl.ds(three, (POOL - 1) * three)], x_send)
    await_bytes(got_picks.at[pl.ds(1, POOL - 1)], pick_send)
    await_bytes(parts, part_send)
    await_bytes(answers.at[pl.ds(three, (POOL - 1) * three)], answer_send)


def compiler_params(collective_id):
    return pltpu.CompilerParams(
        collective_id=collective_id, has_side_effects=True, vmem_limit_bytes=60 << 20
    )


def shards(
    normed_input,
    base_query_output,
    adapter_down_weight,
    adapter_up_weight,
    row_adapter_index,
    paged_key_cache,
    paged_value_cache,
    step_token_keys,
    step_token_values,
    row_page_table,
    lengths,
):
    rows = row_adapter_index.shape[0]
    features = normed_input.shape[2]
    held, rank = adapter_up_weight.shape[:2]
    count, page, kv, head = paged_key_cache.shape
    ctx = page * row_page_table.shape[1]
    width = held * rank
    me = lax.axis_index("pool")
    bf16, f32 = jnp.bfloat16, jnp.float32
    smem = pl.BlockSpec(memory_space=pltpu.SMEM)
    vmem = pl.BlockSpec(memory_space=pltpu.VMEM)
    anywhere = pl.BlockSpec(memory_space=pl.ANY)
    dma = pltpu.SemaphoreType.DMA

    order = jnp.arange(rows, dtype=jnp.int32)
    positions = jnp.arange(POOL, dtype=jnp.int32)
    lane = jnp.arange(LANES, dtype=jnp.int32)

    def among(same):
        return jnp.sum((same & (order[None, :] < order[:, None])).astype(jnp.int32), axis=1)

    arrays = (
        normed_input,
        base_query_output,
        adapter_down_weight.transpose(1, 2, 0).reshape(width, features),
        adapter_up_weight.reshape(width, features),
        paged_key_cache.reshape(count, page * kv, head),
        paged_value_cache.reshape(count, page * kv, head),
        step_token_keys.reshape(STEPS * rows * kv, head),
        step_token_values.reshape(STEPS * rows * kv, head),
    )
    staged = [
        pltpu.VMEM((STEPS, rows, features), bf16),
        pltpu.VMEM((STEPS, rows, features), bf16),
    ]
    staged_rest = [
        pltpu.VMEM((count, page * kv, head), bf16),
        pltpu.VMEM((count, page * kv, head), bf16),
        pltpu.VMEM((STEPS * rows * kv, head), bf16),
        pltpu.VMEM((STEPS * rows * kv, head), bf16),
        pltpu.VMEM((STEPS * rows, BLOCK, LANES), bf16),
        pltpu.VMEM((STEPS * rows * BLOCK, LANES), f32),
        pltpu.VMEM((STEPS * rows * BLOCK, LANES), f32),
    ]
    result = jax.ShapeDtypeStruct((STEPS, rows, features), bf16)
    cost = pl.CostEstimate(
        flops=3_000_000_000, bytes_accessed=12_000_000, transcendentals=1_000_000
    )

    def blocks(n):
        return pltpu.VMEM((n, BLOCK, LANES), bf16)

    def weights(n):
        return [pltpu.VMEM((n * width, features), bf16)] * 2

    def shared_chip():
        chip = row_adapter_index // (C * held)
        rank_there = among(chip[None, :] == chip[:, None])
        core_of = jnp.arange(C, dtype=jnp.int32)
        there = position(me, chip[:, None] * C + core_of[None, :])
        whole = jnp.sum(jnp.where(rank_there[:, None] == core_of[None, :], there, 0), axis=1)
        whole = jnp.where(rank_there < C, whole, -1)
        to_whole = positions[:, None] == whole[None, :]
        third = rank_there == C
        to_third = jnp.any(positions[:, None, None] == there[None, :, :], axis=2) & third[None, :]
        slot_row = jnp.sum(jnp.where(to_whole, order[None, :], 0), axis=1)
        third_row = jnp.sum(jnp.where(to_third, order[None, :], 0), axis=1)
        row_answer = jnp.where(
            rank_there[None, :] < C,
            jnp.maximum(whole, 0)[None, :] * THREE + core_of[:, None],
            there.T * THREE + STEPS,
        )
        named = row_adapter_index % (C * held)
        picks = sum(
            jnp.dot(
                aimed.astype(bf16),
                (named[:, None] + i * C * held == lane[None, :]).astype(bf16),
                preferred_element_type=f32,
            )
            for i, aimed in enumerate((to_whole, to_third))
        )
        full = jnp.any(rank_there > C).astype(f32)
        picks = jnp.where(lane[None, :] == 2 * C * held, full, picks)
        n = POOL * THREE
        brows = BATCH * THREE
        return pl.pallas_call(
            functools.partial(shared_chip_kernel, rows, ctx, page),
            out_shape=(result, jax.ShapeDtypeStruct((1, 1), jnp.int32)),
            in_specs=[smem] * 5 + [vmem] + [anywhere] * 8,
            out_specs=(vmem, smem),
            scratch_shapes=staged
            + weights(C)
            + staged_rest
            + [
                blocks(n),
                blocks(n),
                pltpu.VMEM((POOL, 1, LANES), f32),
                pltpu.VMEM((BATCHES, brows, C * width), bf16),
                pltpu.VMEM((BATCHES, brows, LANES), f32),
                pltpu.VMEM((BATCHES, TP - 1, brows, LANES), f32),
                pltpu.VMEM((brows * BLOCK, LANES), f32),
                blocks(n),
                blocks(n),
                dma((8,)),
                dma((2,)),
                dma((2,)),
                dma,
                dma((BATCHES,)),
                dma,
                dma((BATCHES,)),
                dma,
                dma((BATCHES,)),
                dma,
                dma,
            ],
            compiler_params=compiler_params(0),
            cost_estimate=cost,
            name="shared_chip_and_attention",
        )(
            slot_row,
            third_row,
            row_answer,
            row_page_table.T,
            lengths,
            picks.reshape(POOL, 1, LANES),
            *arrays,
        )

    def every_slot():
        owner = row_adapter_index // held
        earlier = among(owner[None, :] == owner[:, None])
        toward = position(me, owner)
        wanted = earlier[:, None] * held + row_adapter_index[:, None] % held == lane[None, :]
        aimed = positions[:, None] == toward[None, :]
        picks = jnp.dot(aimed.astype(bf16), wanted.astype(bf16), preferred_element_type=f32)
        row_slot = toward * SLOTS + earlier
        place = jnp.arange(POOL * SLOTS, dtype=jnp.int32)[:, None] == row_slot[None, :]
        slot_row = jnp.sum(jnp.where(place, order[None, :], 0), axis=1)
        n = POOL * PER
        grows = GROUP * PER
        return pl.pallas_call(
            functools.partial(every_slot_kernel, rows, ctx, page),
            out_shape=result,
            in_specs=[smem] * 4 + [vmem] + [anywhere] * 8,
            out_specs=vmem,
            scratch_shapes=staged
            + weights(1)
            + staged_rest
            + [
                blocks(n),
                blocks(n),
                pltpu.VMEM((POOL, 1, LANES), f32),
                pltpu.VMEM((GROUPS, grows, width), bf16),
                pltpu.VMEM((GROUPS, grows, LANES), f32),
                pltpu.VMEM((GROUPS, TP - 1, grows, LANES), f32),
                pltpu.VMEM((grows * BLOCK, LANES), f32),
                blocks(n),
                blocks(n),
                dma((8,)),
                dma,
                dma((GROUPS,)),
                dma,
                dma((GROUPS,)),
                dma,
                dma((GROUPS,)),
                dma,
                dma,
            ],
            compiler_params=compiler_params(1),
            cost_estimate=cost,
            name="every_slot_and_attention",
        )(
            slot_row,
            toward[None, :] * PER + earlier[None, :] + SLOTS * jnp.arange(STEPS)[:, None],
            row_page_table.T,
            lengths,
            picks.reshape(POOL, 1, LANES),
            *arrays,
        )

    attended, full = shared_chip()
    return lax.cond(full[0, 0] > 0, every_slot, lambda: attended)


def solution(mesh):
    placed = (
        P(None, "pool", "tp"),
        P(None, "pool", "tp"),
        P("tp", "pool", None),
        P("pool", None, "tp"),
        P("pool"),
        P("pool", None, "tp", None),
        P("pool", None, "tp", None),
        P(None, "pool", "tp", None),
        P(None, "pool", "tp", None),
        P("pool", None),
        P("pool"),
    )
    return jax.shard_map(
        shards, mesh=mesh, in_specs=placed, out_specs=P(None, "pool", "tp"), check_vma=False
    )
```

```python
import functools

import jax
import jax.numpy as jnp
from jax import lax
from jax.experimental import pallas as pl
from jax.experimental.pallas import tpu as pltpu
from jax.sharding import PartitionSpec as P

ADAPTER_SCALE = 0.5
LOG2_E = 1.4426950408889634
MESH = pl.DeviceIdType.MESH
Y, Z, C = 4, 8, 2
POOL = Y * Z * C
TP = 4
GROUP = 8
GROUPS = POOL // GROUP
BATCH = 16
BATCHES = POOL // BATCH
THREE = 3
STEPS = 2
SLOTS = 2
PER = STEPS * SLOTS
BLOCK = 16
LANES = 128


def offsets(k):
    return k // (Z * C), k % Z, (k // Z) % C


def ahead(me, k):
    dy, dz, dc = offsets(k)
    y, z, c = me // (Z * C), (me // C) % Z, me % C
    return (((y + dy) % Y) * Z + (z + dz) % Z) * C + (c + dc) % C


def behind(me, k):
    dy, dz, dc = offsets(k)
    y, z, c = me // (Z * C), (me // C) % Z, me % C
    return (((y + Y - dy) % Y) * Z + (z + Z - dz) % Z) * C + (c + C - dc) % C


def position(me, other):
    y, z, c = me // (Z * C), (me // C) % Z, me % C
    oy, oz, oc = other // (Z * C), (other // C) % Z, other % C
    dy, dz, dc = (oy - y + Y) % Y, (oz - z + Z) % Z, (oc - c + C) % C
    return (dy * C + dc) * Z + dz


def greet_all(me, my_tp):
    barrier = pltpu.get_barrier_semaphore()

    def greet(k, _):
        pl.semaphore_signal(
            barrier, inc=1, device_id={"pool": ahead(me, k)}, device_id_type=MESH
        )
        return 0

    lax.fori_loop(1, POOL, greet, 0)
    for t in range(1, TP):
        pl.semaphore_signal(
            barrier, inc=1, device_id={"tp": (my_tp + t) % TP}, device_id_type=MESH
        )
    return barrier


def start_loads(pairs, sems):
    loads = [pltpu.make_async_copy(src, dst, sems.at[i]) for i, (src, dst) in enumerate(pairs)]
    for load in loads:
        load.start()
    return loads


def to_blocks(rows, src, dst):
    for s in range(STEPS):
        for c in range(BLOCK):
            dst[pl.ds(s * rows * BLOCK + c, rows, stride=BLOCK), :] = src[
                s, :, c * LANES : (c + 1) * LANES
            ].astype(jnp.float32)


def await_bytes(ref, sem):
    pltpu.make_async_copy(ref, ref, sem).wait()


def attend(
    rows,
    ctx,
    page,
    row_answer,
    pages,
    lengths,
    keys,
    values,
    new_keys,
    new_values,
    base_blocks,
    returned,
    out_blocks,
    out_ref,
):
    heads = BLOCK
    f32, bf16 = jnp.float32, jnp.bfloat16
    kv = 2
    old = ctx * kv
    near = BLOCK // kv
    mine = STEPS * heads
    col = lax.broadcasted_iota(jnp.int32, (mine, old), 1)
    query_row = lax.broadcasted_iota(jnp.int32, (mine, old), 0)
    old_key = jnp.where((query_row % heads) // (heads // kv) == col % kv, col, 1 << 20)
    shape = (near * mine, STEPS * BLOCK)
    col = lax.broadcasted_iota(jnp.int32, shape, 1)
    query_row = lax.broadcasted_iota(jnp.int32, shape, 0)
    fresh_live = (
        ((col % BLOCK) // kv == query_row // mine)
        & (col // BLOCK <= (query_row % mine) // heads)
        & (col % kv == (query_row % heads) // (heads // kv))
    )
    per_row = ctx // page
    scale = LOG2_E / (LANES**0.5)

    def eight_rows(tile, _):
        queries = []
        for i in range(near):
            r = tile * near + i
            for s in range(STEPS):
                at = pl.multiple_of((s * rows + r) * BLOCK, BLOCK)
                delta = returned[row_answer[s, r]].astype(f32)
                queries.append((base_blocks[pl.ds(at, BLOCK), :] + delta).astype(bf16))
        query = jnp.concatenate(queries, axis=0)
        fresh_at = [
            pl.ds(pl.multiple_of(s * rows * kv + tile * BLOCK, BLOCK), BLOCK)
            for s in range(STEPS)
        ]
        new_key = jnp.concatenate([new_keys[at, :] for at in fresh_at], axis=0)
        new_value = jnp.concatenate([new_values[at, :] for at in fresh_at], axis=0)
        transposed = (((1,), (1,)), ((), ()))
        fresh = lax.dot_general(query, new_key, transposed, preferred_element_type=f32)
        fresh = jnp.where(fresh_live, fresh, -1e30)
        scores = []
        for i in range(near):
            r = tile * near + i
            key = jnp.concatenate([keys[pages[p, r]] for p in range(per_row)], axis=0)
            part = lax.dot_general(
                query[i * mine : (i + 1) * mine], key, transposed, preferred_element_type=f32
            )
            scores.append(jnp.where(old_key < lengths[0, r] * kv, part, -1e30))
        scores = jnp.concatenate(scores, axis=0)
        top = jnp.maximum(
            jnp.max(scores, axis=-1, keepdims=True), jnp.max(fresh, axis=-1, keepdims=True)
        )
        e_old = jnp.exp2((scores - top) * scale)
        e_new = jnp.exp2((fresh - top) * scale)
        total = jnp.sum(e_old, axis=-1, keepdims=True) + jnp.sum(e_new, axis=-1, keepdims=True)
        share = 1.0 / total
        w_old = (e_old * share).astype(bf16)
        w_new = (e_new * share).astype(bf16)
        result = jnp.dot(w_new, new_value, preferred_element_type=f32)
        for i in range(near):
            r = tile * near + i
            value = jnp.concatenate([values[pages[p, r]] for p in range(per_row)], axis=0)
            both = result[i * mine : (i + 1) * mine] + jnp.dot(
                w_old[i * mine : (i + 1) * mine], value, preferred_element_type=f32
            )
            for s in range(STEPS):
                at = pl.multiple_of((s * rows + r) * BLOCK, BLOCK)
                out_blocks[pl.ds(at, BLOCK), :] = both[s * heads : (s + 1) * heads]
        return 0

    lax.fori_loop(0, rows // near, eight_rows, 0, unroll=2)

    for s in range(STEPS):
        for c in range(BLOCK):
            out_ref[s, :, c * LANES : (c + 1) * LANES] = out_blocks[
                pl.ds(s * rows * BLOCK + c, rows, stride=BLOCK), :
            ].astype(bf16)


def every_slot_kernel(
    rows,
    ctx,
    page,
    slot_row,
    row_answer,
    pages,
    lengths,
    picks,
    x_hbm,
    base_hbm,
    down_hbm,
    up_hbm,
    key_hbm,
    value_hbm,
    new_key_hbm,
    new_value_hbm,
    out_ref,
    x_in,
    base_in,
    down,
    up,
    keys,
    values,
    new_keys,
    new_values,
    x_blocks,
    base_blocks,
    out_blocks,
    sent,
    got,
    got_picks,
    masks,
    own_part,
    parts,
    wide,
    answers,
    returned,
    local_sems,
    x_send,
    x_recv,
    pick_send,
    pick_recv,
    part_send,
    part_recv,
    answer_send,
    answer_recv,
):
    me = lax.axis_index("pool")
    my_tp = lax.axis_index("tp")
    f32, bf16 = jnp.float32, jnp.bfloat16

    barrier = greet_all(me, my_tp)
    loads = start_loads(
        (
            (x_hbm, x_in),
            (down_hbm, down),
            (up_hbm, up),
            (base_hbm, base_in),
            (key_hbm, keys),
            (value_hbm, values),
            (new_key_hbm, new_keys),
            (new_value_hbm, new_values),
        ),
        local_sems,
    )
    loads[0].wait()
    to_blocks(rows, x_in, base_blocks)
    x_blocks[...] = base_blocks[...].astype(bf16).reshape(STEPS * rows, BLOCK, LANES)

    pl.semaphore_wait(barrier, POOL - 1 + TP - 1)

    def message(k, src, dst, send_sem, recv_sem, to):
        return pltpu.make_async_remote_copy(
            src_ref=src.at[pl.ds(k * PER, PER)],
            dst_ref=dst.at[pl.ds(k * PER, PER)],
            send_sem=send_sem,
            recv_sem=recv_sem,
            device_id={"pool": to},
            device_id_type=MESH,
        )

    def blocks_of(k, dst):
        for j in range(SLOTS):
            row = slot_row[k * SLOTS + j]
            for s in range(STEPS):
                dst[k * PER + s * SLOTS + j] = x_blocks[row + s * rows]

    def send_row(k, _):
        blocks_of(k, sent)
        to = ahead(me, k)
        pltpu.make_async_remote_copy(
            src_ref=picks.at[k],
            dst_ref=got_picks.at[k],
            send_sem=pick_send,
            recv_sem=pick_recv.at[k // GROUP],
            device_id={"pool": to},
            device_id_type=MESH,
        ).start()
        message(k, sent, got, x_send, x_recv.at[k // GROUP], to).start()
        return 0

    lax.fori_loop(1, POOL, send_row, 0)
    blocks_of(0, got)
    got_picks[0] = picks[0]

    loads[1].wait()
    loads[2].wait()

    grows = GROUP * PER
    width = down.shape[0]
    rank = width // 8
    spread = (
        lax.broadcasted_iota(jnp.int32, (grows, GROUP), 0) // PER
        == lax.broadcasted_iota(jnp.int32, (grows, GROUP), 1)
    ).astype(f32)
    lane = lax.broadcasted_iota(jnp.int32, (grows, LANES), 1)
    slot = lax.broadcasted_iota(jnp.int32, (grows, LANES), 0) % SLOTS
    slot_lanes = (lane // 8 == slot).astype(f32)
    widen = (
        lax.broadcasted_iota(jnp.int32, (LANES, width), 0) % 8
        == lax.broadcasted_iota(jnp.int32, (LANES, width), 1) // rank
    ).astype(f32)

    def group_bytes(g, first, ref, per, sem):
        lo, n = g * GROUP * per, GROUP * per
        if first:
            lo, n = per, (GROUP - 1) * per
        part = ref.at[pl.ds(lo, n)]
        pltpu.make_async_copy(part, part, sem).wait()

    def project_down(g, first):
        group_bytes(g, first, got, PER, x_recv.at[g])
        group_bytes(g, first, got_picks, 1, pick_recv.at[g])
        wide[...] = got[pl.ds(g * grows, grows)].reshape(grows * BLOCK, LANES).astype(f32)
        features = jnp.concatenate(
            [wide[pl.ds(c, grows, stride=BLOCK), :] for c in range(BLOCK)], axis=1
        ).astype(bf16)
        product = lax.dot_general(
            features, down[...], (((1,), (1,)), ((), ())), preferred_element_type=f32
        )
        chosen = got_picks[pl.ds(g * GROUP, GROUP)].reshape(GROUP, LANES)
        chosen = jnp.dot(spread, chosen, preferred_element_type=f32) * slot_lanes
        mask = jnp.dot(chosen, widen, preferred_element_type=f32)
        masks[g] = mask.astype(bf16)
        product = product * mask
        part = product[:, :LANES]
        for i in range(1, width // LANES):
            part = part + product[:, i * LANES : (i + 1) * LANES]
        own_part[g] = part
        for t in range(1, TP):
            pltpu.make_async_remote_copy(
                src_ref=own_part.at[g],
                dst_ref=parts.at[g, t - 1],
                send_sem=part_send,
                recv_sem=part_recv.at[g],
                device_id={"tp": (my_tp + t) % TP},
                device_id_type=MESH,
            ).start()

    def project_up(g, first):
        pltpu.make_async_copy(parts.at[g], parts.at[g], part_recv.at[g]).wait()
        u = own_part[g] + parts[g, 0] + parts[g, 1] + parts[g, 2]
        u = u.astype(bf16)
        u = jnp.concatenate([u] * (width // LANES), axis=1) * masks[g]
        delta = jnp.dot(u, up[...], preferred_element_type=f32) * ADAPTER_SCALE
        for c in range(BLOCK):
            wide[pl.ds(c, grows, stride=BLOCK), :] = delta[:, c * LANES : (c + 1) * LANES]
        answers[pl.ds(g * grows, grows)] = (
            wide[...].astype(bf16).reshape(grows, BLOCK, LANES)
        )

        def answer(k, _):
            message(k, answers, returned, answer_send, answer_recv, behind(me, k)).start()
            return 0

        if first:
            returned[pl.ds(0, PER)] = answers[pl.ds(0, PER)]
            lax.fori_loop(1, GROUP, answer, 0)
        else:
            lax.fori_loop(g * GROUP, (g + 1) * GROUP, answer, 0)

    project_down(0, True)
    project_down(1, False)
    project_up(0, True)

    def advance(g, _):
        project_down(g, False)
        project_up(g - 1, False)
        return 0

    lax.fori_loop(2, GROUPS, advance, 0)
    project_up(GROUPS - 1, False)

    for load in loads[3:]:
        load.wait()
    to_blocks(rows, base_in, base_blocks)

    tail = returned.at[pl.ds(PER, (POOL - 1) * PER)]
    pltpu.make_async_copy(tail, tail, answer_recv).wait()

    attend(
        rows,
        ctx,
        page,
        row_answer,
        pages,
        lengths,
        keys,
        values,
        new_keys,
        new_values,
        base_blocks,
        returned,
        out_blocks,
        out_ref,
    )

    others = sent.at[pl.ds(PER, (POOL - 1) * PER)]
    pltpu.make_async_copy(others, others, x_send).wait()
    others = answers.at[pl.ds(PER, (POOL - 1) * PER)]
    pltpu.make_async_copy(others, others, answer_send).wait()
    others = got_picks.at[pl.ds(1, POOL - 1)]
    pltpu.make_async_copy(others, others, pick_send).wait()
    pltpu.make_async_copy(parts, parts, part_send).wait()


def shared_chip_kernel(
    rows,
    ctx,
    page,
    adapter_hbm,
    pages_hbm,
    lengths_hbm,
    x_hbm,
    base_hbm,
    down_hbm,
    up_hbm,
    key_hbm,
    value_hbm,
    new_key_hbm,
    new_value_hbm,
    out_ref,
    full_ref,
    adapters,
    answer_table,
    row_answer,
    pages,
    lengths,
    picks,
    x_in,
    base_in,
    down,
    up,
    keys,
    values,
    new_keys,
    new_values,
    base_blocks,
    out_blocks,
    sent,
    got,
    got_picks,
    masks,
    own_part,
    parts,
    wide,
    answers,
    returned,
    local_sems,
    table_sem,
    weight_send,
    weight_recv,
    x_send,
    x_recv,
    pick_send,
    pick_recv,
    part_send,
    part_recv,
    answer_send,
    answer_recv,
):
    me = lax.axis_index("pool")
    my_tp = lax.axis_index("tp")
    my_core = me % C
    f32, bf16 = jnp.float32, jnp.bfloat16
    three = THREE

    width = down_hbm.shape[0]
    my_part = pl.ds(pl.multiple_of(my_core * width, width), width)
    loads = start_loads(
        (
            (adapter_hbm, adapters),
            (x_hbm, x_in),
            (down_hbm, down.at[my_part]),
            (up_hbm, up.at[my_part]),
            (base_hbm, base_in),
            (key_hbm, keys),
            (value_hbm, values),
            (new_key_hbm, new_keys),
            (new_value_hbm, new_values),
            (pages_hbm, pages),
            (lengths_hbm, lengths),
        ),
        local_sems,
    )
    barrier = greet_all(me, my_tp)

    held = 8
    both = C * held
    rank = width // held
    loads[0].wait()
    i32 = jnp.int32

    def iota(shape, axis):
        return lax.broadcasted_iota(i32, shape, axis)

    square = (rows, rows)
    across = adapters[...]
    down_wards = jnp.sum(
        jnp.where(iota(square, 0) == iota(square, 1), across.astype(f32), 0.0), axis=1, keepdims=True
    ).astype(i32)
    same_chip = across // both == down_wards // both
    order = jnp.sum(
        (same_chip & (iota(square, 0) < iota(square, 1))).astype(f32), axis=0, keepdims=True
    ).astype(i32)
    chip = across // both
    dy = (chip // Z + Y - me // (Z * C)) % Y
    dz = (chip % Z + Z - (me // C) % Z) % Z
    chip_at = dy * (Z * C) + dz
    whole = jnp.where(order < C, chip_at + (order + C - my_core) % C * Z, -1)
    third = jnp.where(order == C, chip_at, -1)
    full = jnp.max((order > C).astype(f32), axis=1, keepdims=True)
    for s in range(STEPS):
        split = (chip_at + (s + C - my_core) % C * Z) * three + STEPS
        answer_table[s : s + 1, :rows] = jnp.where(order < C, whole * three + s, split)
    table = pltpu.make_async_copy(answer_table, row_answer, table_sem)
    table.start()

    spots = (POOL, rows)
    to_whole = (iota(spots, 0) == whole).astype(f32)
    to_third = (iota(spots, 0) - (iota(spots, 0) // Z) % C * Z == third).astype(f32)
    named = down_wards % both
    lanes = iota((rows, LANES), 1)
    listed = (
        jnp.dot(to_whole, (lanes == named).astype(f32), preferred_element_type=f32)
        + jnp.dot(to_third, (lanes == named + both).astype(f32), preferred_element_type=f32)
        + jnp.where(iota((POOL, LANES), 1) == 2 * both, full, 0.0)
    )
    picks[...] = listed.reshape(POOL, 1, LANES)
    loads[1].wait()

    brows = BATCH * three

    def build(b, dst):
        shape = (brows, rows)
        line = iota(shape, 0)
        at, part = line // three + b * BATCH, line % three
        its_core = (my_core + (at // Z) % C) % C
        its_chip = at - (at // Z) % C * Z
        total = None
        for s in range(STEPS):
            hit = ((at == whole) & (part == s)) | (
                (its_chip == third) & (part == STEPS) & (its_core == s)
            )
            term = jnp.dot(hit.astype(bf16), x_in[s], preferred_element_type=f32)
            total = term if total is None else total + term
        for c in range(BLOCK):
            wide[pl.ds(c, brows, stride=BLOCK), :] = total[:, c * LANES : (c + 1) * LANES]
        dst[pl.ds(b * brows, brows)] = wide[...].astype(bf16).reshape(brows, BLOCK, LANES)

    build(0, sent)
    pl.semaphore_wait(barrier, POOL - 1 + TP - 1)

    def push(src, dst, send_sem, recv_sem, to):
        pltpu.make_async_remote_copy(
            src_ref=src,
            dst_ref=dst,
            send_sem=send_sem,
            recv_sem=recv_sem,
            device_id={"pool": to},
            device_id_type=MESH,
        ).start()

    def message(ref, k, n):
        return ref.at[pl.ds(k * n, n)]

    def send_row(k, _):
        to, b = ahead(me, k), k // BATCH
        push(message(picks, k, 1), message(got_picks, k, 1), pick_send, pick_recv.at[b], to)
        push(message(sent, k, three), message(got, k, three), x_send, x_recv.at[b], to)
        return 0

    other = ahead(me, Z)
    lax.fori_loop(1, BATCH, send_row, 0)
    push(down_hbm, down.at[my_part], weight_send.at[0], weight_recv.at[0], other)
    for b in range(1, BATCHES):
        build(b, sent)
        lax.fori_loop(b * BATCH, (b + 1) * BATCH, send_row, 0)
        if b == 1:
            push(up_hbm, up.at[my_part], weight_send.at[1], weight_recv.at[1], other)
    got[pl.ds(0, three)] = sent[pl.ds(0, three)]
    got_picks[0] = picks[0]

    loads[4].wait()
    to_blocks(rows, base_in, base_blocks)

    spread = (
        lax.broadcasted_iota(jnp.int32, (brows, BATCH), 0) // three
        == lax.broadcasted_iota(jnp.int32, (brows, BATCH), 1)
    ).astype(f32)
    slot_lanes = (
        lax.broadcasted_iota(jnp.int32, (brows, LANES), 1) // both
        == (lax.broadcasted_iota(jnp.int32, (brows, LANES), 0) % three) // STEPS
    ).astype(f32)
    widen = (
        lax.broadcasted_iota(jnp.int32, (LANES, C * width), 0) % both
        == lax.broadcasted_iota(jnp.int32, (LANES, C * width), 1) // rank
    ).astype(f32)

    def down_batch(b):
        first = 1 if b == 0 else 0
        await_bytes(got_picks.at[pl.ds(b * BATCH + first, BATCH - first)], pick_recv.at[b])
        chosen = got_picks[pl.ds(b * BATCH, BATCH)].reshape(BATCH, LANES)
        chosen = jnp.dot(spread, chosen, preferred_element_type=f32) * slot_lanes
        mask = jnp.dot(chosen, widen, preferred_element_type=f32)
        masks[b] = mask.astype(bf16)
        await_bytes(
            got.at[pl.ds(b * brows + first * three, brows - first * three)], x_recv.at[b]
        )
        blocks = got[pl.ds(b * brows, brows)]
        wide[...] = blocks.reshape(brows * BLOCK, LANES).astype(f32)
        features = jnp.concatenate(
            [wide[pl.ds(c, brows, stride=BLOCK), :] for c in range(BLOCK)], axis=1
        ).astype(bf16)
        product = lax.dot_general(
            features, down[...], (((1,), (1,)), ((), ())), preferred_element_type=f32
        )
        product = product * mask
        part = product[:, :LANES]
        for i in range(1, C * width // LANES):
            part = part + product[:, i * LANES : (i + 1) * LANES]
        own_part[b] = part
        for t in range(1, TP):
            pltpu.make_async_remote_copy(
                src_ref=own_part.at[b],
                dst_ref=parts.at[b, t - 1],
                send_sem=part_send,
                recv_sem=part_recv.at[b],
                device_id={"tp": (my_tp + t) % TP},
                device_id_type=MESH,
            ).start()

    def up_batch(b):
        await_bytes(parts.at[b], part_recv.at[b])
        u = own_part[b] + parts[b, 0] + parts[b, 1] + parts[b, 2]
        u = jnp.concatenate([u.astype(bf16)] * (C * width // LANES), axis=1) * masks[b]
        delta = jnp.dot(u, up[...], preferred_element_type=f32) * ADAPTER_SCALE
        for c in range(BLOCK):
            wide[pl.ds(c, brows, stride=BLOCK), :] = delta[:, c * LANES : (c + 1) * LANES]
        answers[pl.ds(b * brows, brows)] = wide[...].astype(bf16).reshape(brows, BLOCK, LANES)

        def answer(k, _):
            push(
                message(answers, k, three),
                message(returned, k, three),
                answer_send,
                answer_recv,
                behind(me, k),
            )
            return 0

        if b == 0:
            returned[pl.ds(0, three)] = answers[pl.ds(0, three)]
        lax.fori_loop(max(b * BATCH, 1), (b + 1) * BATCH, answer, 0)

    loads[2].wait()
    await_bytes(down.at[my_part], weight_recv.at[0])
    down_batch(0)
    down_batch(1)
    loads[3].wait()
    await_bytes(up.at[my_part], weight_recv.at[1])
    up_batch(0)
    for b in range(2, BATCHES):
        down_batch(b)
        up_batch(b - 1)
    up_batch(BATCHES - 1)

    full_ref[0, 0] = jnp.max(got_picks[...].reshape(POOL, LANES)[:, 2 * both]).astype(jnp.int32)
    table.wait()
    for load in loads[5:]:
        load.wait()
    await_bytes(returned.at[pl.ds(three, (POOL - 1) * three)], answer_recv)
    attend(
        rows,
        ctx,
        page,
        row_answer,
        pages,
        lengths,
        keys,
        values,
        new_keys,
        new_values,
        base_blocks,
        returned,
        out_blocks,
        out_ref,
    )

    await_bytes(down.at[my_part], weight_send.at[0])
    await_bytes(up.at[my_part], weight_send.at[1])
    await_bytes(sent.at[pl.ds(three, (POOL - 1) * three)], x_send)
    await_bytes(got_picks.at[pl.ds(1, POOL - 1)], pick_send)
    await_bytes(parts, part_send)
    await_bytes(answers.at[pl.ds(three, (POOL - 1) * three)], answer_send)


def compiler_params(collective_id):
    return pltpu.CompilerParams(
        collective_id=collective_id, has_side_effects=True, vmem_limit_bytes=60 << 20
    )


def shards(
    normed_input,
    base_query_output,
    adapter_down_weight,
    adapter_up_weight,
    row_adapter_index,
    paged_key_cache,
    paged_value_cache,
    step_token_keys,
    step_token_values,
    row_page_table,
    lengths,
):
    rows = row_adapter_index.shape[0]
    features = normed_input.shape[2]
    held, rank = adapter_up_weight.shape[:2]
    count, page, kv, head = paged_key_cache.shape
    ctx = page * row_page_table.shape[1]
    width = held * rank
    me = lax.axis_index("pool")
    bf16, f32 = jnp.bfloat16, jnp.float32
    smem = pl.BlockSpec(memory_space=pltpu.SMEM)
    vmem = pl.BlockSpec(memory_space=pltpu.VMEM)
    anywhere = pl.BlockSpec(memory_space=pl.ANY)
    dma = pltpu.SemaphoreType.DMA

    arrays = (
        normed_input,
        base_query_output,
        adapter_down_weight.transpose(1, 2, 0).reshape(width, features),
        adapter_up_weight.reshape(width, features),
        paged_key_cache.reshape(count, page * kv, head),
        paged_value_cache.reshape(count, page * kv, head),
        step_token_keys.reshape(STEPS * rows * kv, head),
        step_token_values.reshape(STEPS * rows * kv, head),
    )
    staged = [
        pltpu.VMEM((STEPS, rows, features), bf16),
        pltpu.VMEM((STEPS, rows, features), bf16),
    ]
    staged_rest = [
        pltpu.VMEM((count, page * kv, head), bf16),
        pltpu.VMEM((count, page * kv, head), bf16),
        pltpu.VMEM((STEPS * rows * kv, head), bf16),
        pltpu.VMEM((STEPS * rows * kv, head), bf16),
        pltpu.VMEM((STEPS * rows, BLOCK, LANES), bf16),
        pltpu.VMEM((STEPS * rows * BLOCK, LANES), f32),
        pltpu.VMEM((STEPS * rows * BLOCK, LANES), f32),
    ]
    result = jax.ShapeDtypeStruct((STEPS, rows, features), bf16)
    cost = pl.CostEstimate(
        flops=3_000_000_000, bytes_accessed=12_000_000, transcendentals=1_000_000
    )

    def blocks(n):
        return pltpu.VMEM((n, BLOCK, LANES), bf16)

    def weights(n):
        return [pltpu.VMEM((n * width, features), bf16)] * 2

    def shared_chip():
        n = POOL * THREE
        brows = BATCH * THREE
        return pl.pallas_call(
            functools.partial(shared_chip_kernel, rows, ctx, page),
            out_shape=(result, jax.ShapeDtypeStruct((1, 1), jnp.int32)),
            in_specs=[anywhere] * 11,
            out_specs=(vmem, smem),
            scratch_shapes=[
                pltpu.VMEM((1, rows), jnp.int32),
                pltpu.VMEM((8, LANES), jnp.int32),
                pltpu.SMEM((8, LANES), jnp.int32),
                pltpu.SMEM(row_page_table.T.shape, jnp.int32),
                pltpu.SMEM((1, rows), jnp.int32),
                pltpu.VMEM((POOL, 1, LANES), f32),
            ]
            + staged
            + weights(C)
            + staged_rest[:4]
            + staged_rest[5:]
            + [
                blocks(n),
                blocks(n),
                pltpu.VMEM((POOL, 1, LANES), f32),
                pltpu.VMEM((BATCHES, brows, C * width), bf16),
                pltpu.VMEM((BATCHES, brows, LANES), f32),
                pltpu.VMEM((BATCHES, TP - 1, brows, LANES), f32),
                pltpu.VMEM((brows * BLOCK, LANES), f32),
                blocks(n),
                blocks(n),
                dma((11,)),
                dma,
                dma((2,)),
                dma((2,)),
                dma,
                dma((BATCHES,)),
                dma,
                dma((BATCHES,)),
                dma,
                dma((BATCHES,)),
                dma,
                dma,
            ],
            compiler_params=compiler_params(0),
            cost_estimate=cost,
            name="shared_chip_and_attention",
        )(
            row_adapter_index.reshape(1, rows),
            row_page_table.T,
            lengths.reshape(1, rows),
            *arrays,
        )

    def every_slot():
        order = jnp.arange(rows, dtype=jnp.int32)
        positions = jnp.arange(POOL, dtype=jnp.int32)
        lane = jnp.arange(LANES, dtype=jnp.int32)
        owner = row_adapter_index // held
        ahead_of = (owner[None, :] == owner[:, None]) & (order[None, :] < order[:, None])
        earlier = jnp.sum(ahead_of.astype(jnp.int32), axis=1)
        toward = position(me, owner)
        wanted = earlier[:, None] * held + row_adapter_index[:, None] % held == lane[None, :]
        aimed = positions[:, None] == toward[None, :]
        picks = jnp.dot(aimed.astype(bf16), wanted.astype(bf16), preferred_element_type=f32)
        row_slot = toward * SLOTS + earlier
        place = jnp.arange(POOL * SLOTS, dtype=jnp.int32)[:, None] == row_slot[None, :]
        slot_row = jnp.sum(jnp.where(place, order[None, :], 0), axis=1)
        n = POOL * PER
        grows = GROUP * PER
        return pl.pallas_call(
            functools.partial(every_slot_kernel, rows, ctx, page),
            out_shape=result,
            in_specs=[smem] * 4 + [vmem] + [anywhere] * 8,
            out_specs=vmem,
            scratch_shapes=staged
            + weights(1)
            + staged_rest
            + [
                blocks(n),
                blocks(n),
                pltpu.VMEM((POOL, 1, LANES), f32),
                pltpu.VMEM((GROUPS, grows, width), bf16),
                pltpu.VMEM((GROUPS, grows, LANES), f32),
                pltpu.VMEM((GROUPS, TP - 1, grows, LANES), f32),
                pltpu.VMEM((grows * BLOCK, LANES), f32),
                blocks(n),
                blocks(n),
                dma((8,)),
                dma,
                dma((GROUPS,)),
                dma,
                dma((GROUPS,)),
                dma,
                dma((GROUPS,)),
                dma,
                dma,
            ],
            compiler_params=compiler_params(1),
            cost_estimate=cost,
            name="every_slot_and_attention",
        )(
            slot_row,
            toward[None, :] * PER + earlier[None, :] + SLOTS * jnp.arange(STEPS)[:, None],
            row_page_table.T,
            lengths.reshape(1, rows),
            picks.reshape(POOL, 1, LANES),
            *arrays,
        )

    attended, full = shared_chip()
    return lax.cond(full[0, 0] > 0, every_slot, lambda: attended)


def solution(mesh):
    placed = (
        P(None, "pool", "tp"),
        P(None, "pool", "tp"),
        P("tp", "pool", None),
        P("pool", None, "tp"),
        P("pool"),
        P("pool", None, "tp", None),
        P("pool", None, "tp", None),
        P(None, "pool", "tp", None),
        P(None, "pool", "tp", None),
        P("pool", None),
        P("pool"),
    )
    return jax.shard_map(
        shards, mesh=mesh, in_specs=placed, out_specs=P(None, "pool", "tp"), check_vma=False
    )
```

```python
import functools

import jax
import jax.numpy as jnp
from jax import lax
from jax.experimental import pallas as pl
from jax.experimental.pallas import tpu as pltpu
from jax.sharding import PartitionSpec as P

ADAPTER_SCALE = 0.5
LOG2_E = 1.4426950408889634
MESH = pl.DeviceIdType.MESH
Y, Z, C = 4, 8, 2
POOL = Y * Z * C
TP = 4
GROUP = 8
GROUPS = POOL // GROUP
BATCH = 16
BATCHES = POOL // BATCH
THREE = 3
STEPS = 2
SLOTS = 2
PER = STEPS * SLOTS
BLOCK = 16
LANES = 128


def offsets(k):
    return k // (Z * C), k % Z, (k // Z) % C


def ahead(me, k):
    dy, dz, dc = offsets(k)
    y, z, c = me // (Z * C), (me // C) % Z, me % C
    return (((y + dy) % Y) * Z + (z + dz) % Z) * C + (c + dc) % C


def behind(me, k):
    dy, dz, dc = offsets(k)
    y, z, c = me // (Z * C), (me // C) % Z, me % C
    return (((y + Y - dy) % Y) * Z + (z + Z - dz) % Z) * C + (c + C - dc) % C


def position(me, other):
    y, z, c = me // (Z * C), (me // C) % Z, me % C
    oy, oz, oc = other // (Z * C), (other // C) % Z, other % C
    dy, dz, dc = (oy - y + Y) % Y, (oz - z + Z) % Z, (oc - c + C) % C
    return (dy * C + dc) * Z + dz


def greet_all(me, my_tp):
    barrier = pltpu.get_barrier_semaphore()

    def greet(k, _):
        pl.semaphore_signal(
            barrier, inc=1, device_id={"pool": ahead(me, k)}, device_id_type=MESH
        )
        return 0

    lax.fori_loop(1, POOL, greet, 0)
    for t in range(1, TP):
        pl.semaphore_signal(
            barrier, inc=1, device_id={"tp": (my_tp + t) % TP}, device_id_type=MESH
        )
    return barrier


def start_loads(pairs, sems):
    loads = [pltpu.make_async_copy(src, dst, sems.at[i]) for i, (src, dst) in enumerate(pairs)]
    for load in loads:
        load.start()
    return loads


def to_blocks(rows, src, dst):
    for s in range(STEPS):
        for c in range(BLOCK):
            dst[pl.ds(s * rows * BLOCK + c, rows, stride=BLOCK), :] = src[
                s, :, c * LANES : (c + 1) * LANES
            ].astype(jnp.float32)


def await_bytes(ref, sem):
    pltpu.make_async_copy(ref, ref, sem).wait()


def attend(
    rows,
    ctx,
    page,
    row_answer,
    pages,
    lengths,
    keys,
    values,
    new_keys,
    new_values,
    base_blocks,
    returned,
    out_blocks,
    out_ref,
):
    heads = BLOCK
    f32, bf16 = jnp.float32, jnp.bfloat16
    kv = 2
    old = ctx * kv
    near = BLOCK // kv
    mine = STEPS * heads
    col = lax.broadcasted_iota(jnp.int32, (mine, old), 1)
    query_row = lax.broadcasted_iota(jnp.int32, (mine, old), 0)
    old_key = jnp.where((query_row % heads) // (heads // kv) == col % kv, col, 1 << 20)
    shape = (near * mine, STEPS * BLOCK)
    col = lax.broadcasted_iota(jnp.int32, shape, 1)
    query_row = lax.broadcasted_iota(jnp.int32, shape, 0)
    fresh_live = (
        ((col % BLOCK) // kv == query_row // mine)
        & (col // BLOCK <= (query_row % mine) // heads)
        & (col % kv == (query_row % heads) // (heads // kv))
    )
    per_row = ctx // page
    scale = LOG2_E / (LANES**0.5)

    def eight_rows(tile, _):
        queries = []
        for i in range(near):
            r = tile * near + i
            for s in range(STEPS):
                at = pl.multiple_of((s * rows + r) * BLOCK, BLOCK)
                delta = returned[row_answer[s, r]].astype(f32)
                queries.append((base_blocks[pl.ds(at, BLOCK), :] + delta).astype(bf16))
        query = jnp.concatenate(queries, axis=0)
        fresh_at = [
            pl.ds(pl.multiple_of(s * rows * kv + tile * BLOCK, BLOCK), BLOCK)
            for s in range(STEPS)
        ]
        new_key = jnp.concatenate([new_keys[at, :] for at in fresh_at], axis=0)
        new_value = jnp.concatenate([new_values[at, :] for at in fresh_at], axis=0)
        transposed = (((1,), (1,)), ((), ()))
        fresh = lax.dot_general(query, new_key, transposed, preferred_element_type=f32)
        fresh = jnp.where(fresh_live, fresh, -1e30)
        scores = []
        for i in range(near):
            r = tile * near + i
            key = jnp.concatenate([keys[pages[p, r]] for p in range(per_row)], axis=0)
            part = lax.dot_general(
                query[i * mine : (i + 1) * mine], key, transposed, preferred_element_type=f32
            )
            scores.append(jnp.where(old_key < lengths[0, r] * kv, part, -1e30))
        scores = jnp.concatenate(scores, axis=0)
        top = jnp.maximum(
            jnp.max(scores, axis=-1, keepdims=True), jnp.max(fresh, axis=-1, keepdims=True)
        )
        e_old = jnp.exp2((scores - top) * scale)
        e_new = jnp.exp2((fresh - top) * scale)
        total = jnp.sum(e_old, axis=-1, keepdims=True) + jnp.sum(e_new, axis=-1, keepdims=True)
        share = 1.0 / total
        w_old = (e_old * share).astype(bf16)
        w_new = (e_new * share).astype(bf16)
        result = jnp.dot(w_new, new_value, preferred_element_type=f32)
        for i in range(near):
            r = tile * near + i
            value = jnp.concatenate([values[pages[p, r]] for p in range(per_row)], axis=0)
            both = result[i * mine : (i + 1) * mine] + jnp.dot(
                w_old[i * mine : (i + 1) * mine], value, preferred_element_type=f32
            )
            for s in range(STEPS):
                at = pl.multiple_of((s * rows + r) * BLOCK, BLOCK)
                out_blocks[pl.ds(at, BLOCK), :] = both[s * heads : (s + 1) * heads]
        return 0

    lax.fori_loop(0, rows // near, eight_rows, 0, unroll=6)

    for s in range(STEPS):
        for c in range(BLOCK):
            out_ref[s, :, c * LANES : (c + 1) * LANES] = out_blocks[
                pl.ds(s * rows * BLOCK + c, rows, stride=BLOCK), :
            ].astype(bf16)


def every_slot_kernel(
    rows,
    ctx,
    page,
    slot_row,
    row_answer,
    pages,
    lengths,
    picks,
    x_hbm,
    base_hbm,
    down_hbm,
    up_hbm,
    key_hbm,
    value_hbm,
    new_key_hbm,
    new_value_hbm,
    out_ref,
    x_in,
    base_in,
    down,
    up,
    keys,
    values,
    new_keys,
    new_values,
    x_blocks,
    base_blocks,
    out_blocks,
    sent,
    got,
    got_picks,
    masks,
    own_part,
    parts,
    wide,
    answers,
    returned,
    local_sems,
    x_send,
    x_recv,
    pick_send,
    pick_recv,
    part_send,
    part_recv,
    answer_send,
    answer_recv,
):
    me = lax.axis_index("pool")
    my_tp = lax.axis_index("tp")
    f32, bf16 = jnp.float32, jnp.bfloat16

    barrier = greet_all(me, my_tp)
    loads = start_loads(
        (
            (x_hbm, x_in),
            (down_hbm, down),
            (up_hbm, up),
            (base_hbm, base_in),
            (key_hbm, keys),
            (value_hbm, values),
            (new_key_hbm, new_keys),
            (new_value_hbm, new_values),
        ),
        local_sems,
    )
    loads[0].wait()
    to_blocks(rows, x_in, base_blocks)
    x_blocks[...] = base_blocks[...].astype(bf16).reshape(STEPS * rows, BLOCK, LANES)

    pl.semaphore_wait(barrier, POOL - 1 + TP - 1)

    def message(k, src, dst, send_sem, recv_sem, to):
        return pltpu.make_async_remote_copy(
            src_ref=src.at[pl.ds(k * PER, PER)],
            dst_ref=dst.at[pl.ds(k * PER, PER)],
            send_sem=send_sem,
            recv_sem=recv_sem,
            device_id={"pool": to},
            device_id_type=MESH,
        )

    def blocks_of(k, dst):
        for j in range(SLOTS):
            row = slot_row[k * SLOTS + j]
            for s in range(STEPS):
                dst[k * PER + s * SLOTS + j] = x_blocks[row + s * rows]

    def send_row(k, _):
        blocks_of(k, sent)
        to = ahead(me, k)
        pltpu.make_async_remote_copy(
            src_ref=picks.at[k],
            dst_ref=got_picks.at[k],
            send_sem=pick_send,
            recv_sem=pick_recv.at[k // GROUP],
            device_id={"pool": to},
            device_id_type=MESH,
        ).start()
        message(k, sent, got, x_send, x_recv.at[k // GROUP], to).start()
        return 0

    lax.fori_loop(1, POOL, send_row, 0)
    blocks_of(0, got)
    got_picks[0] = picks[0]

    loads[1].wait()
    loads[2].wait()

    grows = GROUP * PER
    width = down.shape[0]
    rank = width // 8
    spread = (
        lax.broadcasted_iota(jnp.int32, (grows, GROUP), 0) // PER
        == lax.broadcasted_iota(jnp.int32, (grows, GROUP), 1)
    ).astype(f32)
    lane = lax.broadcasted_iota(jnp.int32, (grows, LANES), 1)
    slot = lax.broadcasted_iota(jnp.int32, (grows, LANES), 0) % SLOTS
    slot_lanes = (lane // 8 == slot).astype(f32)
    widen = (
        lax.broadcasted_iota(jnp.int32, (LANES, width), 0) % 8
        == lax.broadcasted_iota(jnp.int32, (LANES, width), 1) // rank
    ).astype(f32)

    def group_bytes(g, first, ref, per, sem):
        lo, n = g * GROUP * per, GROUP * per
        if first:
            lo, n = per, (GROUP - 1) * per
        part = ref.at[pl.ds(lo, n)]
        pltpu.make_async_copy(part, part, sem).wait()

    def project_down(g, first):
        group_bytes(g, first, got, PER, x_recv.at[g])
        group_bytes(g, first, got_picks, 1, pick_recv.at[g])
        wide[...] = got[pl.ds(g * grows, grows)].reshape(grows * BLOCK, LANES).astype(f32)
        features = jnp.concatenate(
            [wide[pl.ds(c, grows, stride=BLOCK), :] for c in range(BLOCK)], axis=1
        ).astype(bf16)
        product = lax.dot_general(
            features, down[...], (((1,), (1,)), ((), ())), preferred_element_type=f32
        )
        chosen = got_picks[pl.ds(g * GROUP, GROUP)].reshape(GROUP, LANES)
        chosen = jnp.dot(spread, chosen, preferred_element_type=f32) * slot_lanes
        mask = jnp.dot(chosen, widen, preferred_element_type=f32)
        masks[g] = mask.astype(bf16)
        product = product * mask
        part = product[:, :LANES]
        for i in range(1, width // LANES):
            part = part + product[:, i * LANES : (i + 1) * LANES]
        own_part[g] = part
        for t in range(1, TP):
            pltpu.make_async_remote_copy(
                src_ref=own_part.at[g],
                dst_ref=parts.at[g, t - 1],
                send_sem=part_send,
                recv_sem=part_recv.at[g],
                device_id={"tp": (my_tp + t) % TP},
                device_id_type=MESH,
            ).start()

    def project_up(g, first):
        pltpu.make_async_copy(parts.at[g], parts.at[g], part_recv.at[g]).wait()
        u = own_part[g] + parts[g, 0] + parts[g, 1] + parts[g, 2]
        u = u.astype(bf16)
        u = jnp.concatenate([u] * (width // LANES), axis=1) * masks[g]
        delta = jnp.dot(u, up[...], preferred_element_type=f32) * ADAPTER_SCALE
        for c in range(BLOCK):
            wide[pl.ds(c, grows, stride=BLOCK), :] = delta[:, c * LANES : (c + 1) * LANES]
        answers[pl.ds(g * grows, grows)] = (
            wide[...].astype(bf16).reshape(grows, BLOCK, LANES)
        )

        def answer(k, _):
            message(k, answers, returned, answer_send, answer_recv, behind(me, k)).start()
            return 0

        if first:
            returned[pl.ds(0, PER)] = answers[pl.ds(0, PER)]
            lax.fori_loop(1, GROUP, answer, 0)
        else:
            lax.fori_loop(g * GROUP, (g + 1) * GROUP, answer, 0)

    project_down(0, True)
    project_down(1, False)
    project_up(0, True)

    def advance(g, _):
        project_down(g, False)
        project_up(g - 1, False)
        return 0

    lax.fori_loop(2, GROUPS, advance, 0)
    project_up(GROUPS - 1, False)

    for load in loads[3:]:
        load.wait()
    to_blocks(rows, base_in, base_blocks)

    tail = returned.at[pl.ds(PER, (POOL - 1) * PER)]
    pltpu.make_async_copy(tail, tail, answer_recv).wait()

    attend(
        rows,
        ctx,
        page,
        row_answer,
        pages,
        lengths,
        keys,
        values,
        new_keys,
        new_values,
        base_blocks,
        returned,
        out_blocks,
        out_ref,
    )

    others = sent.at[pl.ds(PER, (POOL - 1) * PER)]
    pltpu.make_async_copy(others, others, x_send).wait()
    others = answers.at[pl.ds(PER, (POOL - 1) * PER)]
    pltpu.make_async_copy(others, others, answer_send).wait()
    others = got_picks.at[pl.ds(1, POOL - 1)]
    pltpu.make_async_copy(others, others, pick_send).wait()
    pltpu.make_async_copy(parts, parts, part_send).wait()


def shared_chip_kernel(
    rows,
    ctx,
    page,
    adapter_hbm,
    pages_hbm,
    lengths_hbm,
    x_hbm,
    base_hbm,
    down_hbm,
    up_hbm,
    key_hbm,
    value_hbm,
    new_key_hbm,
    new_value_hbm,
    out_ref,
    full_ref,
    adapters,
    answer_table,
    row_answer,
    pages,
    lengths,
    picks,
    x_in,
    base_in,
    down,
    up,
    keys,
    values,
    new_keys,
    new_values,
    base_blocks,
    out_blocks,
    sent,
    got,
    got_picks,
    masks,
    own_part,
    parts,
    wide,
    answers,
    returned,
    local_sems,
    table_sem,
    weight_send,
    weight_recv,
    x_send,
    x_recv,
    pick_send,
    pick_recv,
    part_send,
    part_recv,
    answer_send,
    answer_recv,
):
    me = lax.axis_index("pool")
    my_tp = lax.axis_index("tp")
    my_core = me % C
    f32, bf16 = jnp.float32, jnp.bfloat16
    three = THREE

    width = down_hbm.shape[0]
    my_part = pl.ds(pl.multiple_of(my_core * width, width), width)
    loads = start_loads(
        (
            (adapter_hbm, adapters),
            (x_hbm, x_in),
            (down_hbm, down.at[my_part]),
            (up_hbm, up.at[my_part]),
            (base_hbm, base_in),
            (key_hbm, keys),
            (value_hbm, values),
            (new_key_hbm, new_keys),
            (new_value_hbm, new_values),
            (pages_hbm, pages),
            (lengths_hbm, lengths),
        ),
        local_sems,
    )
    barrier = greet_all(me, my_tp)

    held = 8
    both = C * held
    rank = width // held
    loads[0].wait()
    i32 = jnp.int32

    def iota(shape, axis):
        return lax.broadcasted_iota(i32, shape, axis)

    square = (rows, rows)
    across = adapters[...]
    down_wards = jnp.sum(
        jnp.where(iota(square, 0) == iota(square, 1), across.astype(f32), 0.0), axis=1, keepdims=True
    ).astype(i32)
    same_chip = across // both == down_wards // both
    order = jnp.sum(
        (same_chip & (iota(square, 0) < iota(square, 1))).astype(f32), axis=0, keepdims=True
    ).astype(i32)
    chip = across // both
    dy = (chip // Z + Y - me // (Z * C)) % Y
    dz = (chip % Z + Z - (me // C) % Z) % Z
    chip_at = dy * (Z * C) + dz
    whole = jnp.where(order < C, chip_at + (order + C - my_core) % C * Z, -1)
    third = jnp.where(order == C, chip_at, -1)
    full = jnp.max((order > C).astype(f32), axis=1, keepdims=True)
    for s in range(STEPS):
        split = (chip_at + (s + C - my_core) % C * Z) * three + STEPS
        answer_table[s : s + 1, :rows] = jnp.where(order < C, whole * three + s, split)
    table = pltpu.make_async_copy(answer_table, row_answer, table_sem)
    table.start()

    spots = (POOL, rows)
    to_whole = (iota(spots, 0) == whole).astype(f32)
    to_third = (iota(spots, 0) - (iota(spots, 0) // Z) % C * Z == third).astype(f32)
    named = down_wards % both
    lanes = iota((rows, LANES), 1)
    listed = (
        jnp.dot(to_whole, (lanes == named).astype(f32), preferred_element_type=f32)
        + jnp.dot(to_third, (lanes == named + both).astype(f32), preferred_element_type=f32)
        + jnp.where(iota((POOL, LANES), 1) == 2 * both, full, 0.0)
    )
    picks[...] = listed.reshape(POOL, 1, LANES)
    loads[1].wait()

    brows = BATCH * three

    def build(b, dst):
        shape = (brows, rows)
        line = iota(shape, 0)
        at, part = line // three + b * BATCH, line % three
        its_core = (my_core + (at // Z) % C) % C
        its_chip = at - (at // Z) % C * Z
        total = None
        for s in range(STEPS):
            hit = ((at == whole) & (part == s)) | (
                (its_chip == third) & (part == STEPS) & (its_core == s)
            )
            term = jnp.dot(hit.astype(bf16), x_in[s], preferred_element_type=f32)
            total = term if total is None else total + term
        for c in range(BLOCK):
            wide[pl.ds(c, brows, stride=BLOCK), :] = total[:, c * LANES : (c + 1) * LANES]
        dst[pl.ds(b * brows, brows)] = wide[...].astype(bf16).reshape(brows, BLOCK, LANES)

    build(0, sent)
    pl.semaphore_wait(barrier, POOL - 1 + TP - 1)

    def push(src, dst, send_sem, recv_sem, to):
        pltpu.make_async_remote_copy(
            src_ref=src,
            dst_ref=dst,
            send_sem=send_sem,
            recv_sem=recv_sem,
            device_id={"pool": to},
            device_id_type=MESH,
        ).start()

    def message(ref, k, n):
        return ref.at[pl.ds(k * n, n)]

    def send_row(k, _):
        to, b = ahead(me, k), k // BATCH
        push(message(picks, k, 1), message(got_picks, k, 1), pick_send, pick_recv.at[b], to)
        push(message(sent, k, three), message(got, k, three), x_send, x_recv.at[b], to)
        return 0

    other = ahead(me, Z)
    lax.fori_loop(1, BATCH, send_row, 0)
    push(down_hbm, down.at[my_part], weight_send.at[0], weight_recv.at[0], other)
    for b in range(1, BATCHES):
        build(b, sent)
        lax.fori_loop(b * BATCH, (b + 1) * BATCH, send_row, 0)
        if b == 1:
            push(up_hbm, up.at[my_part], weight_send.at[1], weight_recv.at[1], other)
    got[pl.ds(0, three)] = sent[pl.ds(0, three)]
    got_picks[0] = picks[0]

    loads[4].wait()
    to_blocks(rows, base_in, base_blocks)

    spread = (
        lax.broadcasted_iota(jnp.int32, (brows, BATCH), 0) // three
        == lax.broadcasted_iota(jnp.int32, (brows, BATCH), 1)
    ).astype(f32)
    slot_lanes = (
        lax.broadcasted_iota(jnp.int32, (brows, LANES), 1) // both
        == (lax.broadcasted_iota(jnp.int32, (brows, LANES), 0) % three) // STEPS
    ).astype(f32)
    widen = (
        lax.broadcasted_iota(jnp.int32, (LANES, C * width), 0) % both
        == lax.broadcasted_iota(jnp.int32, (LANES, C * width), 1) // rank
    ).astype(f32)

    def down_batch(b):
        first = 1 if b == 0 else 0
        await_bytes(got_picks.at[pl.ds(b * BATCH + first, BATCH - first)], pick_recv.at[b])
        chosen = got_picks[pl.ds(b * BATCH, BATCH)].reshape(BATCH, LANES)
        chosen = jnp.dot(spread, chosen, preferred_element_type=f32) * slot_lanes
        mask = jnp.dot(chosen, widen, preferred_element_type=f32)
        masks[b] = mask.astype(bf16)
        await_bytes(
            got.at[pl.ds(b * brows + first * three, brows - first * three)], x_recv.at[b]
        )
        blocks = got[pl.ds(b * brows, brows)]
        wide[...] = blocks.reshape(brows * BLOCK, LANES).astype(f32)
        features = jnp.concatenate(
            [wide[pl.ds(c, brows, stride=BLOCK), :] for c in range(BLOCK)], axis=1
        ).astype(bf16)
        product = lax.dot_general(
            features, down[...], (((1,), (1,)), ((), ())), preferred_element_type=f32
        )
        product = product * mask
        part = product[:, :LANES]
        for i in range(1, C * width // LANES):
            part = part + product[:, i * LANES : (i + 1) * LANES]
        own_part[b] = part
        for t in range(1, TP):
            pltpu.make_async_remote_copy(
                src_ref=own_part.at[b],
                dst_ref=parts.at[b, t - 1],
                send_sem=part_send,
                recv_sem=part_recv.at[b],
                device_id={"tp": (my_tp + t) % TP},
                device_id_type=MESH,
            ).start()

    def up_batch(b):
        await_bytes(parts.at[b], part_recv.at[b])
        u = own_part[b] + parts[b, 0] + parts[b, 1] + parts[b, 2]
        u = jnp.concatenate([u.astype(bf16)] * (C * width // LANES), axis=1) * masks[b]
        delta = jnp.dot(u, up[...], preferred_element_type=f32) * ADAPTER_SCALE
        for c in range(BLOCK):
            wide[pl.ds(c, brows, stride=BLOCK), :] = delta[:, c * LANES : (c + 1) * LANES]
        answers[pl.ds(b * brows, brows)] = wide[...].astype(bf16).reshape(brows, BLOCK, LANES)

        def answer(k, _):
            push(
                message(answers, k, three),
                message(returned, k, three),
                answer_send,
                answer_recv,
                behind(me, k),
            )
            return 0

        if b == 0:
            returned[pl.ds(0, three)] = answers[pl.ds(0, three)]
        lax.fori_loop(max(b * BATCH, 1), (b + 1) * BATCH, answer, 0)

    loads[2].wait()
    await_bytes(down.at[my_part], weight_recv.at[0])
    down_batch(0)
    down_batch(1)
    loads[3].wait()
    await_bytes(up.at[my_part], weight_recv.at[1])
    up_batch(0)
    for b in range(2, BATCHES):
        down_batch(b)
        up_batch(b - 1)
    up_batch(BATCHES - 1)

    full_ref[0, 0] = jnp.max(got_picks[...].reshape(POOL, LANES)[:, 2 * both]).astype(jnp.int32)
    table.wait()
    for load in loads[5:]:
        load.wait()
    await_bytes(returned.at[pl.ds(three, (POOL - 1) * three)], answer_recv)
    attend(
        rows,
        ctx,
        page,
        row_answer,
        pages,
        lengths,
        keys,
        values,
        new_keys,
        new_values,
        base_blocks,
        returned,
        out_blocks,
        out_ref,
    )

    await_bytes(down.at[my_part], weight_send.at[0])
    await_bytes(up.at[my_part], weight_send.at[1])
    await_bytes(sent.at[pl.ds(three, (POOL - 1) * three)], x_send)
    await_bytes(got_picks.at[pl.ds(1, POOL - 1)], pick_send)
    await_bytes(parts, part_send)
    await_bytes(answers.at[pl.ds(three, (POOL - 1) * three)], answer_send)


def compiler_params(collective_id):
    return pltpu.CompilerParams(
        collective_id=collective_id, has_side_effects=True, vmem_limit_bytes=60 << 20
    )


def shards(
    normed_input,
    base_query_output,
    adapter_down_weight,
    adapter_up_weight,
    row_adapter_index,
    paged_key_cache,
    paged_value_cache,
    step_token_keys,
    step_token_values,
    row_page_table,
    lengths,
):
    rows = row_adapter_index.shape[0]
    features = normed_input.shape[2]
    held, rank = adapter_up_weight.shape[:2]
    count, page, kv, head = paged_key_cache.shape
    ctx = page * row_page_table.shape[1]
    width = held * rank
    me = lax.axis_index("pool")
    bf16, f32 = jnp.bfloat16, jnp.float32
    smem = pl.BlockSpec(memory_space=pltpu.SMEM)
    vmem = pl.BlockSpec(memory_space=pltpu.VMEM)
    anywhere = pl.BlockSpec(memory_space=pl.ANY)
    dma = pltpu.SemaphoreType.DMA

    arrays = (
        normed_input,
        base_query_output,
        adapter_down_weight.transpose(1, 2, 0).reshape(width, features),
        adapter_up_weight.reshape(width, features),
        paged_key_cache.reshape(count, page * kv, head),
        paged_value_cache.reshape(count, page * kv, head),
        step_token_keys.reshape(STEPS * rows * kv, head),
        step_token_values.reshape(STEPS * rows * kv, head),
    )
    staged = [
        pltpu.VMEM((STEPS, rows, features), bf16),
        pltpu.VMEM((STEPS, rows, features), bf16),
    ]
    staged_rest = [
        pltpu.VMEM((count, page * kv, head), bf16),
        pltpu.VMEM((count, page * kv, head), bf16),
        pltpu.VMEM((STEPS * rows * kv, head), bf16),
        pltpu.VMEM((STEPS * rows * kv, head), bf16),
        pltpu.VMEM((STEPS * rows, BLOCK, LANES), bf16),
        pltpu.VMEM((STEPS * rows * BLOCK, LANES), f32),
        pltpu.VMEM((STEPS * rows * BLOCK, LANES), f32),
    ]
    result = jax.ShapeDtypeStruct((STEPS, rows, features), bf16)
    cost = pl.CostEstimate(
        flops=3_000_000_000, bytes_accessed=12_000_000, transcendentals=1_000_000
    )

    def blocks(n):
        return pltpu.VMEM((n, BLOCK, LANES), bf16)

    def weights(n):
        return [pltpu.VMEM((n * width, features), bf16)] * 2

    def shared_chip():
        n = POOL * THREE
        brows = BATCH * THREE
        return pl.pallas_call(
            functools.partial(shared_chip_kernel, rows, ctx, page),
            out_shape=(result, jax.ShapeDtypeStruct((1, 1), jnp.int32)),
            in_specs=[anywhere] * 11,
            out_specs=(vmem, smem),
            scratch_shapes=[
                pltpu.VMEM((1, rows), jnp.int32),
                pltpu.VMEM((8, LANES), jnp.int32),
                pltpu.SMEM((8, LANES), jnp.int32),
                pltpu.SMEM(row_page_table.T.shape, jnp.int32),
                pltpu.SMEM((1, rows), jnp.int32),
                pltpu.VMEM((POOL, 1, LANES), f32),
            ]
            + staged
            + weights(C)
            + staged_rest[:4]
            + staged_rest[5:]
            + [
                blocks(n),
                blocks(n),
                pltpu.VMEM((POOL, 1, LANES), f32),
                pltpu.VMEM((BATCHES, brows, C * width), bf16),
                pltpu.VMEM((BATCHES, brows, LANES), f32),
                pltpu.VMEM((BATCHES, TP - 1, brows, LANES), f32),
                pltpu.VMEM((brows * BLOCK, LANES), f32),
                blocks(n),
                blocks(n),
                dma((11,)),
                dma,
                dma((2,)),
                dma((2,)),
                dma,
                dma((BATCHES,)),
                dma,
                dma((BATCHES,)),
                dma,
                dma((BATCHES,)),
                dma,
                dma,
            ],
            compiler_params=compiler_params(0),
            cost_estimate=cost,
            name="shared_chip_and_attention",
        )(
            row_adapter_index.reshape(1, rows),
            row_page_table.T,
            lengths.reshape(1, rows),
            *arrays,
        )

    def every_slot():
        order = jnp.arange(rows, dtype=jnp.int32)
        positions = jnp.arange(POOL, dtype=jnp.int32)
        lane = jnp.arange(LANES, dtype=jnp.int32)
        owner = row_adapter_index // held
        ahead_of = (owner[None, :] == owner[:, None]) & (order[None, :] < order[:, None])
        earlier = jnp.sum(ahead_of.astype(jnp.int32), axis=1)
        toward = position(me, owner)
        wanted = earlier[:, None] * held + row_adapter_index[:, None] % held == lane[None, :]
        aimed = positions[:, None] == toward[None, :]
        picks = jnp.dot(aimed.astype(bf16), wanted.astype(bf16), preferred_element_type=f32)
        row_slot = toward * SLOTS + earlier
        place = jnp.arange(POOL * SLOTS, dtype=jnp.int32)[:, None] == row_slot[None, :]
        slot_row = jnp.sum(jnp.where(place, order[None, :], 0), axis=1)
        n = POOL * PER
        grows = GROUP * PER
        return pl.pallas_call(
            functools.partial(every_slot_kernel, rows, ctx, page),
            out_shape=result,
            in_specs=[smem] * 4 + [vmem] + [anywhere] * 8,
            out_specs=vmem,
            scratch_shapes=staged
            + weights(1)
            + staged_rest
            + [
                blocks(n),
                blocks(n),
                pltpu.VMEM((POOL, 1, LANES), f32),
                pltpu.VMEM((GROUPS, grows, width), bf16),
                pltpu.VMEM((GROUPS, grows, LANES), f32),
                pltpu.VMEM((GROUPS, TP - 1, grows, LANES), f32),
                pltpu.VMEM((grows * BLOCK, LANES), f32),
                blocks(n),
                blocks(n),
                dma((8,)),
                dma,
                dma((GROUPS,)),
                dma,
                dma((GROUPS,)),
                dma,
                dma((GROUPS,)),
                dma,
                dma,
            ],
            compiler_params=compiler_params(1),
            cost_estimate=cost,
            name="every_slot_and_attention",
        )(
            slot_row,
            toward[None, :] * PER + earlier[None, :] + SLOTS * jnp.arange(STEPS)[:, None],
            row_page_table.T,
            lengths.reshape(1, rows),
            picks.reshape(POOL, 1, LANES),
            *arrays,
        )

    attended, full = shared_chip()
    return lax.cond(full[0, 0] > 0, every_slot, lambda: attended)


def solution(mesh):
    placed = (
        P(None, "pool", "tp"),
        P(None, "pool", "tp"),
        P("tp", "pool", None),
        P("pool", None, "tp"),
        P("pool"),
        P("pool", None, "tp", None),
        P("pool", None, "tp", None),
        P(None, "pool", "tp", None),
        P(None, "pool", "tp", None),
        P("pool", None),
        P("pool"),
    )
    return jax.shard_map(
        shards, mesh=mesh, in_specs=placed, out_specs=P(None, "pool", "tp"), check_vma=False
    )
```

```python
import functools

import jax
import jax.numpy as jnp
from jax import lax
from jax.experimental import pallas as pl
from jax.experimental.pallas import tpu as pltpu
from jax.sharding import PartitionSpec as P

ADAPTER_SCALE = 0.5
LOG2_E = 1.4426950408889634
MESH = pl.DeviceIdType.MESH
Y, Z, C = 4, 8, 2
POOL = Y * Z * C
TP = 4
GROUP = 8
GROUPS = POOL // GROUP
BATCH = 16
BATCHES = POOL // BATCH
THREE = 3
STEPS = 2
SLOTS = 2
PER = STEPS * SLOTS
BLOCK = 16
LANES = 128


def offsets(k):
    return k // (Z * C), k % Z, (k // Z) % C


def ahead(me, k):
    dy, dz, dc = offsets(k)
    y, z, c = me // (Z * C), (me // C) % Z, me % C
    return (((y + dy) % Y) * Z + (z + dz) % Z) * C + (c + dc) % C


def behind(me, k):
    dy, dz, dc = offsets(k)
    y, z, c = me // (Z * C), (me // C) % Z, me % C
    return (((y + Y - dy) % Y) * Z + (z + Z - dz) % Z) * C + (c + C - dc) % C


def position(me, other):
    y, z, c = me // (Z * C), (me // C) % Z, me % C
    oy, oz, oc = other // (Z * C), (other // C) % Z, other % C
    dy, dz, dc = (oy - y + Y) % Y, (oz - z + Z) % Z, (oc - c + C) % C
    return (dy * C + dc) * Z + dz


def greet_all(me, my_tp):
    barrier = pltpu.get_barrier_semaphore()

    def greet(k, _):
        pl.semaphore_signal(
            barrier, inc=1, device_id={"pool": ahead(me, k)}, device_id_type=MESH
        )
        return 0

    lax.fori_loop(1, POOL, greet, 0)
    for t in range(1, TP):
        pl.semaphore_signal(
            barrier, inc=1, device_id={"tp": (my_tp + t) % TP}, device_id_type=MESH
        )
    return barrier


def start_loads(pairs, sems):
    loads = [pltpu.make_async_copy(src, dst, sems.at[i]) for i, (src, dst) in enumerate(pairs)]
    for load in loads:
        load.start()
    return loads


def to_blocks(rows, src, dst):
    for s in range(STEPS):
        for c in range(BLOCK):
            dst[pl.ds(s * rows * BLOCK + c, rows, stride=BLOCK), :] = src[
                s, :, c * LANES : (c + 1) * LANES
            ].astype(jnp.float32)


def await_bytes(ref, sem):
    pltpu.make_async_copy(ref, ref, sem).wait()


def attend(
    rows,
    ctx,
    page,
    row_answer,
    pages,
    lengths,
    keys,
    values,
    new_keys,
    new_values,
    base_blocks,
    returned,
    out_blocks,
    out_ref,
):
    heads = BLOCK
    f32, bf16 = jnp.float32, jnp.bfloat16
    kv = 2
    old = ctx * kv
    near = BLOCK // kv
    mine = STEPS * heads
    col = lax.broadcasted_iota(jnp.int32, (mine, old), 1)
    query_row = lax.broadcasted_iota(jnp.int32, (mine, old), 0)
    old_key = jnp.where((query_row % heads) // (heads // kv) == col % kv, col, 1 << 20)
    shape = (near * mine, STEPS * BLOCK)
    col = lax.broadcasted_iota(jnp.int32, shape, 1)
    query_row = lax.broadcasted_iota(jnp.int32, shape, 0)
    fresh_live = (
        ((col % BLOCK) // kv == query_row // mine)
        & (col // BLOCK <= (query_row % mine) // heads)
        & (col % kv == (query_row % heads) // (heads // kv))
    )
    per_row = ctx // page
    scale = LOG2_E / (LANES**0.5)

    def eight_rows(tile, _):
        queries = []
        for i in range(near):
            r = tile * near + i
            for s in range(STEPS):
                at = pl.multiple_of((s * rows + r) * BLOCK, BLOCK)
                delta = returned[row_answer[s, r]].astype(f32)
                queries.append((base_blocks[pl.ds(at, BLOCK), :] + delta).astype(bf16))
        query = jnp.concatenate(queries, axis=0)
        fresh_at = [
            pl.ds(pl.multiple_of(s * rows * kv + tile * BLOCK, BLOCK), BLOCK)
            for s in range(STEPS)
        ]
        new_key = jnp.concatenate([new_keys[at, :] for at in fresh_at], axis=0)
        new_value = jnp.concatenate([new_values[at, :] for at in fresh_at], axis=0)
        transposed = (((1,), (1,)), ((), ()))
        fresh = lax.dot_general(query, new_key, transposed, preferred_element_type=f32)
        fresh = jnp.where(fresh_live, fresh, -1e30)
        scores = []
        for i in range(near):
            r = tile * near + i
            key = jnp.concatenate([keys[pages[p, r]] for p in range(per_row)], axis=0)
            part = lax.dot_general(
                query[i * mine : (i + 1) * mine], key, transposed, preferred_element_type=f32
            )
            scores.append(jnp.where(old_key < lengths[0, r] * kv, part, -1e30))
        scores = jnp.concatenate(scores, axis=0)
        top = jnp.maximum(
            jnp.max(scores, axis=-1, keepdims=True), jnp.max(fresh, axis=-1, keepdims=True)
        )
        e_old = jnp.exp2((scores - top) * scale)
        e_new = jnp.exp2((fresh - top) * scale)
        total = jnp.sum(e_old, axis=-1, keepdims=True) + jnp.sum(e_new, axis=-1, keepdims=True)
        share = 1.0 / total
        w_old = (e_old * share).astype(bf16)
        w_new = (e_new * share).astype(bf16)
        result = jnp.dot(w_new, new_value, preferred_element_type=f32)
        for i in range(near):
            r = tile * near + i
            value = jnp.concatenate([values[pages[p, r]] for p in range(per_row)], axis=0)
            both = result[i * mine : (i + 1) * mine] + jnp.dot(
                w_old[i * mine : (i + 1) * mine], value, preferred_element_type=f32
            )
            for s in range(STEPS):
                at = pl.multiple_of((s * rows + r) * BLOCK, BLOCK)
                out_blocks[pl.ds(at, BLOCK), :] = both[s * heads : (s + 1) * heads]
        return 0

    lax.fori_loop(0, rows // near, eight_rows, 0, unroll=6)

    for s in range(STEPS):
        for c in range(BLOCK):
            out_ref[s, :, c * LANES : (c + 1) * LANES] = out_blocks[
                pl.ds(s * rows * BLOCK + c, rows, stride=BLOCK), :
            ].astype(bf16)


def every_slot_kernel(
    rows,
    ctx,
    page,
    slot_row,
    row_answer,
    pages,
    lengths,
    picks,
    x_hbm,
    base_hbm,
    down_hbm,
    up_hbm,
    key_hbm,
    value_hbm,
    new_key_hbm,
    new_value_hbm,
    out_ref,
    x_in,
    base_in,
    down,
    up,
    keys,
    values,
    new_keys,
    new_values,
    x_blocks,
    base_blocks,
    out_blocks,
    sent,
    got,
    got_picks,
    masks,
    own_part,
    parts,
    wide,
    answers,
    returned,
    local_sems,
    x_send,
    x_recv,
    pick_send,
    pick_recv,
    part_send,
    part_recv,
    answer_send,
    answer_recv,
):
    me = lax.axis_index("pool")
    my_tp = lax.axis_index("tp")
    f32, bf16 = jnp.float32, jnp.bfloat16

    barrier = greet_all(me, my_tp)
    loads = start_loads(
        (
            (x_hbm, x_in),
            (down_hbm, down),
            (up_hbm, up),
            (base_hbm, base_in),
            (key_hbm, keys),
            (value_hbm, values),
            (new_key_hbm, new_keys),
            (new_value_hbm, new_values),
        ),
        local_sems,
    )
    loads[0].wait()
    to_blocks(rows, x_in, base_blocks)
    x_blocks[...] = base_blocks[...].astype(bf16).reshape(STEPS * rows, BLOCK, LANES)

    pl.semaphore_wait(barrier, POOL - 1 + TP - 1)

    def message(k, src, dst, send_sem, recv_sem, to):
        return pltpu.make_async_remote_copy(
            src_ref=src.at[pl.ds(k * PER, PER)],
            dst_ref=dst.at[pl.ds(k * PER, PER)],
            send_sem=send_sem,
            recv_sem=recv_sem,
            device_id={"pool": to},
            device_id_type=MESH,
        )

    def blocks_of(k, dst):
        for j in range(SLOTS):
            row = slot_row[k * SLOTS + j]
            for s in range(STEPS):
                dst[k * PER + s * SLOTS + j] = x_blocks[row + s * rows]

    def send_row(k, _):
        blocks_of(k, sent)
        to = ahead(me, k)
        pltpu.make_async_remote_copy(
            src_ref=picks.at[k],
            dst_ref=got_picks.at[k],
            send_sem=pick_send,
            recv_sem=pick_recv.at[k // GROUP],
            device_id={"pool": to},
            device_id_type=MESH,
        ).start()
        message(k, sent, got, x_send, x_recv.at[k // GROUP], to).start()
        return 0

    lax.fori_loop(1, POOL, send_row, 0)
    blocks_of(0, got)
    got_picks[0] = picks[0]

    loads[1].wait()
    loads[2].wait()

    grows = GROUP * PER
    width = down.shape[0]
    rank = width // 8
    spread = (
        lax.broadcasted_iota(jnp.int32, (grows, GROUP), 0) // PER
        == lax.broadcasted_iota(jnp.int32, (grows, GROUP), 1)
    ).astype(f32)
    lane = lax.broadcasted_iota(jnp.int32, (grows, LANES), 1)
    slot = lax.broadcasted_iota(jnp.int32, (grows, LANES), 0) % SLOTS
    slot_lanes = (lane // 8 == slot).astype(f32)
    widen = (
        lax.broadcasted_iota(jnp.int32, (LANES, width), 0) % 8
        == lax.broadcasted_iota(jnp.int32, (LANES, width), 1) // rank
    ).astype(f32)

    def group_bytes(g, first, ref, per, sem):
        lo, n = g * GROUP * per, GROUP * per
        if first:
            lo, n = per, (GROUP - 1) * per
        part = ref.at[pl.ds(lo, n)]
        pltpu.make_async_copy(part, part, sem).wait()

    def project_down(g, first):
        group_bytes(g, first, got, PER, x_recv.at[g])
        group_bytes(g, first, got_picks, 1, pick_recv.at[g])
        wide[...] = got[pl.ds(g * grows, grows)].reshape(grows * BLOCK, LANES).astype(f32)
        features = jnp.concatenate(
            [wide[pl.ds(c, grows, stride=BLOCK), :] for c in range(BLOCK)], axis=1
        ).astype(bf16)
        product = lax.dot_general(
            features, down[...], (((1,), (1,)), ((), ())), preferred_element_type=f32
        )
        chosen = got_picks[pl.ds(g * GROUP, GROUP)].reshape(GROUP, LANES)
        chosen = jnp.dot(spread, chosen, preferred_element_type=f32) * slot_lanes
        mask = jnp.dot(chosen, widen, preferred_element_type=f32)
        masks[g] = mask.astype(bf16)
        product = product * mask
        part = product[:, :LANES]
        for i in range(1, width // LANES):
            part = part + product[:, i * LANES : (i + 1) * LANES]
        own_part[g] = part
        for t in range(1, TP):
            pltpu.make_async_remote_copy(
                src_ref=own_part.at[g],
                dst_ref=parts.at[g, t - 1],
                send_sem=part_send,
                recv_sem=part_recv.at[g],
                device_id={"tp": (my_tp + t) % TP},
                device_id_type=MESH,
            ).start()

    def project_up(g, first):
        pltpu.make_async_copy(parts.at[g], parts.at[g], part_recv.at[g]).wait()
        u = own_part[g] + parts[g, 0] + parts[g, 1] + parts[g, 2]
        u = u.astype(bf16)
        u = jnp.concatenate([u] * (width // LANES), axis=1) * masks[g]
        delta = jnp.dot(u, up[...], preferred_element_type=f32) * ADAPTER_SCALE
        for c in range(BLOCK):
            wide[pl.ds(c, grows, stride=BLOCK), :] = delta[:, c * LANES : (c + 1) * LANES]
        answers[pl.ds(g * grows, grows)] = (
            wide[...].astype(bf16).reshape(grows, BLOCK, LANES)
        )

        def answer(k, _):
            message(k, answers, returned, answer_send, answer_recv, behind(me, k)).start()
            return 0

        if first:
            returned[pl.ds(0, PER)] = answers[pl.ds(0, PER)]
            lax.fori_loop(1, GROUP, answer, 0)
        else:
            lax.fori_loop(g * GROUP, (g + 1) * GROUP, answer, 0)

    project_down(0, True)
    project_down(1, False)
    project_up(0, True)

    def advance(g, _):
        project_down(g, False)
        project_up(g - 1, False)
        return 0

    lax.fori_loop(2, GROUPS, advance, 0)
    project_up(GROUPS - 1, False)

    for load in loads[3:]:
        load.wait()
    to_blocks(rows, base_in, base_blocks)

    tail = returned.at[pl.ds(PER, (POOL - 1) * PER)]
    pltpu.make_async_copy(tail, tail, answer_recv).wait()

    attend(
        rows,
        ctx,
        page,
        row_answer,
        pages,
        lengths,
        keys,
        values,
        new_keys,
        new_values,
        base_blocks,
        returned,
        out_blocks,
        out_ref,
    )

    others = sent.at[pl.ds(PER, (POOL - 1) * PER)]
    pltpu.make_async_copy(others, others, x_send).wait()
    others = answers.at[pl.ds(PER, (POOL - 1) * PER)]
    pltpu.make_async_copy(others, others, answer_send).wait()
    others = got_picks.at[pl.ds(1, POOL - 1)]
    pltpu.make_async_copy(others, others, pick_send).wait()
    pltpu.make_async_copy(parts, parts, part_send).wait()


def far_first(i):
    j = i % BATCH
    return i - j + (j % C) * Z + (j // C + 3) % Z


def shared_chip_kernel(
    rows,
    ctx,
    page,
    adapter_hbm,
    pages_hbm,
    lengths_hbm,
    x_hbm,
    base_hbm,
    down_hbm,
    up_hbm,
    key_hbm,
    value_hbm,
    new_key_hbm,
    new_value_hbm,
    out_ref,
    full_ref,
    adapters,
    answer_table,
    row_answer,
    pages,
    lengths,
    picks,
    x_in,
    base_in,
    down,
    up,
    keys,
    values,
    new_keys,
    new_values,
    base_blocks,
    out_blocks,
    sent,
    got,
    got_picks,
    masks,
    own_part,
    parts,
    wide,
    answers,
    returned,
    local_sems,
    table_sem,
    weight_send,
    weight_recv,
    x_send,
    x_recv,
    pick_send,
    pick_recv,
    part_send,
    part_recv,
    answer_send,
    answer_recv,
):
    me = lax.axis_index("pool")
    my_tp = lax.axis_index("tp")
    my_core = me % C
    f32, bf16 = jnp.float32, jnp.bfloat16
    three = THREE

    width = down_hbm.shape[0]
    my_part = pl.ds(pl.multiple_of(my_core * width, width), width)
    loads = start_loads(
        (
            (adapter_hbm, adapters),
            (x_hbm, x_in),
            (down_hbm, down.at[my_part]),
            (up_hbm, up.at[my_part]),
            (base_hbm, base_in),
            (key_hbm, keys),
            (value_hbm, values),
            (new_key_hbm, new_keys),
            (new_value_hbm, new_values),
            (pages_hbm, pages),
            (lengths_hbm, lengths),
        ),
        local_sems,
    )
    barrier = greet_all(me, my_tp)

    held = 8
    both = C * held
    rank = width // held
    loads[0].wait()
    i32 = jnp.int32

    def iota(shape, axis):
        return lax.broadcasted_iota(i32, shape, axis)

    square = (rows, rows)
    across = adapters[...]
    down_wards = jnp.sum(
        jnp.where(iota(square, 0) == iota(square, 1), across.astype(f32), 0.0), axis=1, keepdims=True
    ).astype(i32)
    same_chip = across // both == down_wards // both
    order = jnp.sum(
        (same_chip & (iota(square, 0) < iota(square, 1))).astype(f32), axis=0, keepdims=True
    ).astype(i32)
    chip = across // both
    dy = (chip // Z + Y - me // (Z * C)) % Y
    dz = (chip % Z + Z - (me // C) % Z) % Z
    chip_at = dy * (Z * C) + dz
    whole = jnp.where(order < C, chip_at + (order + C - my_core) % C * Z, -1)
    third = jnp.where(order == C, chip_at, -1)
    full = jnp.max((order > C).astype(f32), axis=1, keepdims=True)
    for s in range(STEPS):
        split = (chip_at + (s + C - my_core) % C * Z) * three + STEPS
        answer_table[s : s + 1, :rows] = jnp.where(order < C, whole * three + s, split)
    table = pltpu.make_async_copy(answer_table, row_answer, table_sem)
    table.start()

    spots = (POOL, rows)
    to_whole = (iota(spots, 0) == whole).astype(f32)
    to_third = (iota(spots, 0) - (iota(spots, 0) // Z) % C * Z == third).astype(f32)
    named = down_wards % both
    lanes = iota((rows, LANES), 1)
    listed = (
        jnp.dot(to_whole, (lanes == named).astype(f32), preferred_element_type=f32)
        + jnp.dot(to_third, (lanes == named + both).astype(f32), preferred_element_type=f32)
        + jnp.where(iota((POOL, LANES), 1) == 2 * both, full, 0.0)
    )
    picks[...] = listed.reshape(POOL, 1, LANES)
    loads[1].wait()

    brows = BATCH * three

    def build(b, dst):
        shape = (brows, rows)
        line = iota(shape, 0)
        at, part = line // three + b * BATCH, line % three
        its_core = (my_core + (at // Z) % C) % C
        its_chip = at - (at // Z) % C * Z
        total = None
        for s in range(STEPS):
            hit = ((at == whole) & (part == s)) | (
                (its_chip == third) & (part == STEPS) & (its_core == s)
            )
            term = jnp.dot(hit.astype(bf16), x_in[s], preferred_element_type=f32)
            total = term if total is None else total + term
        for c in range(BLOCK):
            wide[pl.ds(c, brows, stride=BLOCK), :] = total[:, c * LANES : (c + 1) * LANES]
        dst[pl.ds(b * brows, brows)] = wide[...].astype(bf16).reshape(brows, BLOCK, LANES)

    build(0, sent)
    pl.semaphore_wait(barrier, POOL - 1 + TP - 1)

    def push(src, dst, send_sem, recv_sem, to):
        pltpu.make_async_remote_copy(
            src_ref=src,
            dst_ref=dst,
            send_sem=send_sem,
            recv_sem=recv_sem,
            device_id={"pool": to},
            device_id_type=MESH,
        ).start()

    def message(ref, k, n):
        return ref.at[pl.ds(k * n, n)]

    def send_row(k, _):
        to, b = ahead(me, k), k // BATCH
        push(message(picks, k, 1), message(got_picks, k, 1), pick_send, pick_recv.at[b], to)
        push(message(sent, k, three), message(got, k, three), x_send, x_recv.at[b], to)
        return 0

    other = ahead(me, Z)
    lax.fori_loop(1, BATCH, send_row, 0)
    push(down_hbm, down.at[my_part], weight_send.at[0], weight_recv.at[0], other)
    for b in range(1, BATCHES):
        build(b, sent)
        lax.fori_loop(
            b * BATCH, (b + 1) * BATCH, lambda i, _: send_row(far_first(i), 0), 0
        )
        if b == 1:
            push(up_hbm, up.at[my_part], weight_send.at[1], weight_recv.at[1], other)
    got[pl.ds(0, three)] = sent[pl.ds(0, three)]
    got_picks[0] = picks[0]

    loads[4].wait()
    to_blocks(rows, base_in, base_blocks)

    spread = (
        lax.broadcasted_iota(jnp.int32, (brows, BATCH), 0) // three
        == lax.broadcasted_iota(jnp.int32, (brows, BATCH), 1)
    ).astype(f32)
    slot_lanes = (
        lax.broadcasted_iota(jnp.int32, (brows, LANES), 1) // both
        == (lax.broadcasted_iota(jnp.int32, (brows, LANES), 0) % three) // STEPS
    ).astype(f32)
    widen = (
        lax.broadcasted_iota(jnp.int32, (LANES, C * width), 0) % both
        == lax.broadcasted_iota(jnp.int32, (LANES, C * width), 1) // rank
    ).astype(f32)

    def down_batch(b):
        first = 1 if b == 0 else 0
        await_bytes(got_picks.at[pl.ds(b * BATCH + first, BATCH - first)], pick_recv.at[b])
        chosen = got_picks[pl.ds(b * BATCH, BATCH)].reshape(BATCH, LANES)
        chosen = jnp.dot(spread, chosen, preferred_element_type=f32) * slot_lanes
        mask = jnp.dot(chosen, widen, preferred_element_type=f32)
        masks[b] = mask.astype(bf16)
        await_bytes(
            got.at[pl.ds(b * brows + first * three, brows - first * three)], x_recv.at[b]
        )
        blocks = got[pl.ds(b * brows, brows)]
        wide[...] = blocks.reshape(brows * BLOCK, LANES).astype(f32)
        features = jnp.concatenate(
            [wide[pl.ds(c, brows, stride=BLOCK), :] for c in range(BLOCK)], axis=1
        ).astype(bf16)
        product = lax.dot_general(
            features, down[...], (((1,), (1,)), ((), ())), preferred_element_type=f32
        )
        product = product * mask
        part = product[:, :LANES]
        for i in range(1, C * width // LANES):
            part = part + product[:, i * LANES : (i + 1) * LANES]
        own_part[b] = part
        for t in range(1, TP):
            pltpu.make_async_remote_copy(
                src_ref=own_part.at[b],
                dst_ref=parts.at[b, t - 1],
                send_sem=part_send,
                recv_sem=part_recv.at[b],
                device_id={"tp": (my_tp + t) % TP},
                device_id_type=MESH,
            ).start()

    def up_batch(b):
        await_bytes(parts.at[b], part_recv.at[b])
        u = own_part[b] + parts[b, 0] + parts[b, 1] + parts[b, 2]
        u = jnp.concatenate([u.astype(bf16)] * (C * width // LANES), axis=1) * masks[b]
        delta = jnp.dot(u, up[...], preferred_element_type=f32) * ADAPTER_SCALE
        for c in range(BLOCK):
            wide[pl.ds(c, brows, stride=BLOCK), :] = delta[:, c * LANES : (c + 1) * LANES]
        answers[pl.ds(b * brows, brows)] = wide[...].astype(bf16).reshape(brows, BLOCK, LANES)

        def answer(k, _):
            push(
                message(answers, k, three),
                message(returned, k, three),
                answer_send,
                answer_recv,
                behind(me, k),
            )
            return 0

        if b == 0:
            returned[pl.ds(0, three)] = answers[pl.ds(0, three)]
            lax.fori_loop(1, BATCH, answer, 0)
        else:
            lax.fori_loop(
                b * BATCH, (b + 1) * BATCH, lambda i, _: answer(far_first(i), 0), 0
            )

    loads[2].wait()
    await_bytes(down.at[my_part], weight_recv.at[0])
    down_batch(0)
    down_batch(1)
    loads[3].wait()
    await_bytes(up.at[my_part], weight_recv.at[1])
    up_batch(0)
    for b in range(2, BATCHES):
        down_batch(b)
        up_batch(b - 1)
    up_batch(BATCHES - 1)

    full_ref[0, 0] = jnp.max(got_picks[...].reshape(POOL, LANES)[:, 2 * both]).astype(jnp.int32)
    table.wait()
    for load in loads[5:]:
        load.wait()
    await_bytes(returned.at[pl.ds(three, (POOL - 1) * three)], answer_recv)
    attend(
        rows,
        ctx,
        page,
        row_answer,
        pages,
        lengths,
        keys,
        values,
        new_keys,
        new_values,
        base_blocks,
        returned,
        out_blocks,
        out_ref,
    )

    await_bytes(down.at[my_part], weight_send.at[0])
    await_bytes(up.at[my_part], weight_send.at[1])
    await_bytes(sent.at[pl.ds(three, (POOL - 1) * three)], x_send)
    await_bytes(got_picks.at[pl.ds(1, POOL - 1)], pick_send)
    await_bytes(parts, part_send)
    await_bytes(answers.at[pl.ds(three, (POOL - 1) * three)], answer_send)


def compiler_params(collective_id):
    return pltpu.CompilerParams(
        collective_id=collective_id, has_side_effects=True, vmem_limit_bytes=60 << 20
    )


def shards(
    normed_input,
    base_query_output,
    adapter_down_weight,
    adapter_up_weight,
    row_adapter_index,
    paged_key_cache,
    paged_value_cache,
    step_token_keys,
    step_token_values,
    row_page_table,
    lengths,
):
    rows = row_adapter_index.shape[0]
    features = normed_input.shape[2]
    held, rank = adapter_up_weight.shape[:2]
    count, page, kv, head = paged_key_cache.shape
    ctx = page * row_page_table.shape[1]
    width = held * rank
    me = lax.axis_index("pool")
    bf16, f32 = jnp.bfloat16, jnp.float32
    smem = pl.BlockSpec(memory_space=pltpu.SMEM)
    vmem = pl.BlockSpec(memory_space=pltpu.VMEM)
    anywhere = pl.BlockSpec(memory_space=pl.ANY)
    dma = pltpu.SemaphoreType.DMA

    arrays = (
        normed_input,
        base_query_output,
        adapter_down_weight.transpose(1, 2, 0).reshape(width, features),
        adapter_up_weight.reshape(width, features),
        paged_key_cache.reshape(count, page * kv, head),
        paged_value_cache.reshape(count, page * kv, head),
        step_token_keys.reshape(STEPS * rows * kv, head),
        step_token_values.reshape(STEPS * rows * kv, head),
    )
    staged = [
        pltpu.VMEM((STEPS, rows, features), bf16),
        pltpu.VMEM((STEPS, rows, features), bf16),
    ]
    staged_rest = [
        pltpu.VMEM((count, page * kv, head), bf16),
        pltpu.VMEM((count, page * kv, head), bf16),
        pltpu.VMEM((STEPS * rows * kv, head), bf16),
        pltpu.VMEM((STEPS * rows * kv, head), bf16),
        pltpu.VMEM((STEPS * rows, BLOCK, LANES), bf16),
        pltpu.VMEM((STEPS * rows * BLOCK, LANES), f32),
        pltpu.VMEM((STEPS * rows * BLOCK, LANES), f32),
    ]
    result = jax.ShapeDtypeStruct((STEPS, rows, features), bf16)
    cost = pl.CostEstimate(
        flops=3_000_000_000, bytes_accessed=12_000_000, transcendentals=1_000_000
    )

    def blocks(n):
        return pltpu.VMEM((n, BLOCK, LANES), bf16)

    def weights(n):
        return [pltpu.VMEM((n * width, features), bf16)] * 2

    def shared_chip():
        n = POOL * THREE
        brows = BATCH * THREE
        return pl.pallas_call(
            functools.partial(shared_chip_kernel, rows, ctx, page),
            out_shape=(result, jax.ShapeDtypeStruct((1, 1), jnp.int32)),
            in_specs=[anywhere] * 11,
            out_specs=(vmem, smem),
            scratch_shapes=[
                pltpu.VMEM((1, rows), jnp.int32),
                pltpu.VMEM((8, LANES), jnp.int32),
                pltpu.SMEM((8, LANES), jnp.int32),
                pltpu.SMEM(row_page_table.T.shape, jnp.int32),
                pltpu.SMEM((1, rows), jnp.int32),
                pltpu.VMEM((POOL, 1, LANES), f32),
            ]
            + staged
            + weights(C)
            + staged_rest[:4]
            + staged_rest[5:]
            + [
                blocks(n),
                blocks(n),
                pltpu.VMEM((POOL, 1, LANES), f32),
                pltpu.VMEM((BATCHES, brows, C * width), bf16),
                pltpu.VMEM((BATCHES, brows, LANES), f32),
                pltpu.VMEM((BATCHES, TP - 1, brows, LANES), f32),
                pltpu.VMEM((brows * BLOCK, LANES), f32),
                blocks(n),
                blocks(n),
                dma((11,)),
                dma,
                dma((2,)),
                dma((2,)),
                dma,
                dma((BATCHES,)),
                dma,
                dma((BATCHES,)),
                dma,
                dma((BATCHES,)),
                dma,
                dma,
            ],
            compiler_params=compiler_params(0),
            cost_estimate=cost,
            name="shared_chip_and_attention",
        )(
            row_adapter_index.reshape(1, rows),
            row_page_table.T,
            lengths.reshape(1, rows),
            *arrays,
        )

    def every_slot():
        order = jnp.arange(rows, dtype=jnp.int32)
        positions = jnp.arange(POOL, dtype=jnp.int32)
        lane = jnp.arange(LANES, dtype=jnp.int32)
        owner = row_adapter_index // held
        ahead_of = (owner[None, :] == owner[:, None]) & (order[None, :] < order[:, None])
        earlier = jnp.sum(ahead_of.astype(jnp.int32), axis=1)
        toward = position(me, owner)
        wanted = earlier[:, None] * held + row_adapter_index[:, None] % held == lane[None, :]
        aimed = positions[:, None] == toward[None, :]
        picks = jnp.dot(aimed.astype(bf16), wanted.astype(bf16), preferred_element_type=f32)
        row_slot = toward * SLOTS + earlier
        place = jnp.arange(POOL * SLOTS, dtype=jnp.int32)[:, None] == row_slot[None, :]
        slot_row = jnp.sum(jnp.where(place, order[None, :], 0), axis=1)
        n = POOL * PER
        grows = GROUP * PER
        return pl.pallas_call(
            functools.partial(every_slot_kernel, rows, ctx, page),
            out_shape=result,
            in_specs=[smem] * 4 + [vmem] + [anywhere] * 8,
            out_specs=vmem,
            scratch_shapes=staged
            + weights(1)
            + staged_rest
            + [
                blocks(n),
                blocks(n),
                pltpu.VMEM((POOL, 1, LANES), f32),
                pltpu.VMEM((GROUPS, grows, width), bf16),
                pltpu.VMEM((GROUPS, grows, LANES), f32),
                pltpu.VMEM((GROUPS, TP - 1, grows, LANES), f32),
                pltpu.VMEM((grows * BLOCK, LANES), f32),
                blocks(n),
                blocks(n),
                dma((8,)),
                dma,
                dma((GROUPS,)),
                dma,
                dma((GROUPS,)),
                dma,
                dma((GROUPS,)),
                dma,
                dma,
            ],
            compiler_params=compiler_params(1),
            cost_estimate=cost,
            name="every_slot_and_attention",
        )(
            slot_row,
            toward[None, :] * PER + earlier[None, :] + SLOTS * jnp.arange(STEPS)[:, None],
            row_page_table.T,
            lengths.reshape(1, rows),
            picks.reshape(POOL, 1, LANES),
            *arrays,
        )

    attended, full = shared_chip()
    return lax.cond(full[0, 0] > 0, every_slot, lambda: attended)


def solution(mesh):
    placed = (
        P(None, "pool", "tp"),
        P(None, "pool", "tp"),
        P("tp", "pool", None),
        P("pool", None, "tp"),
        P("pool"),
        P("pool", None, "tp", None),
        P("pool", None, "tp", None),
        P(None, "pool", "tp", None),
        P(None, "pool", "tp", None),
        P("pool", None),
        P("pool"),
    )
    return jax.shard_map(
        shards, mesh=mesh, in_specs=placed, out_specs=P(None, "pool", "tp"), check_vma=False
    )
```
